512 devices in a mesh: gx: 8 (over y), gy: 4 (over x), gz: 16 (over z, core).
Axes of the slice: x: 4, y: 8, z: 8, core: 2. Of those that a mesh axis runs over, the one named last changes fastest.
Arguments:
- source: float32 [256, 256, 512], P('gz', 'gx', 'gy'), may hold values from -6 to 6
- conductivity: float32 [256, 256, 512], P('gz', 'gx', 'gy'), may hold values from 0.25 to 4
Outputs:
- correction: float32 [256, 256, 512], P('gz', 'gx', 'gy')
- residual: float32 [256, 256, 512], P('gz', 'gx', 'gy')
The draws below stay inside these ranges and needn't reach their ends.
All inputs are finite; a program needn't handle non-finite values.
Results may differ from the reference program's by a relative error of at most 0.0003.
Values sent between devices are 32-bit elements; how exact they have to be, the bound alone decides.
A program may use at most 128 MiB of HBM per device.

```python
import math
import jax
import jax.numpy as jnp
from jax import lax

LEVELS = 7
PRE = 1
POST = 1
BOTTOM = 8
NZ = 256
NX = 256
NY = 512


def draw_source(key, part):
    key = jax.random.fold_in(key, 7)
    values = jnp.clip(jax.random.normal(key, (NZ, NX, NY), jnp.float32), -6.0, 6.0)
    return values


def steps_of(key, shape, split, least, top_value):
    def one(axis_at, parts):
        steps = jax.random.uniform(jax.random.fold_in(jax.random.fold_in(key, 6), axis_at), (parts,), jnp.float32, least / len(split), top_value / len(split))
        return jnp.repeat(jnp.exp(steps), shape[axis_at] // parts).reshape((-1,) + (1,) * (len(shape) - axis_at - 1))

    gain = one(*split[0])
    for cut in split[1:]:
        gain = gain * one(*cut)
    return gain


def setup_inputs(seed: int = 0) -> dict:
    keys = jax.random.split(jax.random.key(seed), 3)
    return {
        "source": draw_source(jax.random.fold_in(keys[2], 71), 0),
        "conductivity": jnp.clip(jnp.exp(math.log(4.0) - 2.7725887 * jax.random.uniform(keys[1], (NZ, NX, NY), jnp.float32) ** steps_of(keys[1], (NZ, NX, NY), ((0, 16), (1, 8), (2, 4)), -0.2, 0.2)), 0.25, 4.0),
    }


OMEGA = 2.0 / 3.0


def crop(field, margin):
    if margin == 0:
        return field
    return field[margin:-margin, margin:-margin, margin:-margin]


def operate(field, weights, scale):
    centre = crop(field, 1)
    inner = crop(weights, 1)
    extent = centre.shape
    total = jnp.zeros_like(centre)
    diagonal = jnp.zeros_like(centre)
    for dimension in range(3):
        for offset in (0, 2):
            starts = [1, 1, 1]
            starts[dimension] = offset
            limits = [starts[0] + extent[0], starts[1] + extent[1], starts[2] + extent[2]]
            neighbour = lax.slice(field, starts, limits)
            weight_near = lax.slice(weights, starts, limits)
            flux_weight = 0.5 * (inner + weight_near)
            total = total + flux_weight * (centre - neighbour)
            diagonal = diagonal + flux_weight
    return scale * total, scale * diagonal


def relax(field, source, weights, scale):
    applied, diagonal = operate(field, weights, scale)
    safe = jnp.where(diagonal > 0.0, diagonal, 1.0)
    return crop(field, 1) + OMEGA * (source - applied) / safe


def restrict(block):
    layers, rows_count, columns = block.shape
    return block.reshape(layers // 2, 2, rows_count // 2, 2, columns // 2, 2).sum(axis=(1, 3, 5)) * 0.125


def prolong(block):
    return jnp.repeat(jnp.repeat(jnp.repeat(block, 2, 0), 2, 1), 2, 2)


def cycle(source, weights, level):
    scale = 0.25 ** level
    wide_weight = jnp.pad(weights, 1)
    field = jnp.zeros_like(source)
    if level == LEVELS - 1:
        for sweep in range(BOTTOM):
            field = relax(jnp.pad(field, 1), source, wide_weight, scale)
        return field
    for sweep in range(PRE):
        field = relax(jnp.pad(field, 1), source, wide_weight, scale)
    applied = operate(jnp.pad(field, 1), wide_weight, scale)[0]
    coarse = cycle(restrict(source - applied), restrict(weights), level + 1)
    field = field + prolong(coarse)
    for sweep in range(POST):
        field = relax(jnp.pad(field, 1), source, wide_weight, scale)
    return field


def reference(source, conductivity):
    correction = cycle(source, conductivity, 0)
    applied = operate(jnp.pad(correction, 1), jnp.pad(conductivity, 1), 1.0)[0]
    return correction, source - applied
```

```python
import jax
import jax.numpy as jnp
from jax import lax
from jax.experimental import pallas as pl
from jax.experimental.pallas import tpu as pltpu
from jax.sharding import PartitionSpec as P

MESH = pl.DeviceIdType.MESH
AXES = ("gx", "gy", "gz")
OMEGA = 2.0 / 3.0
LANES = 128
F32 = jnp.float32

FINE = ((16, 32), (8, 16), (4, 8), (2, 4))
COARSE = ((16, 16, 4), (8, 8, 8), (4, 4, 16))
SWAP_FIELDS = ("w0", "w1", "w2", "w3", "v0", "v1", "v2", "v3", "c3", "c2", "c1", "c0", "r0")


def padded_rows(rows):
    return max(rows, 8)


def lane_of(shape):
    return lax.broadcasted_iota(jnp.int32, shape, len(shape) - 1)


def row_of(shape):
    return lax.broadcasted_iota(jnp.int32, shape, len(shape) - 2)


def loop(count, body, carry):
    if count <= 4:
        for i in range(count):
            carry = body(i, carry)
        return carry
    return lax.fori_loop(0, count, body, carry, unroll=2)


def shift_lanes(x, amount):
    amount = lax.rem(amount + LANES, LANES) if not isinstance(amount, int) else amount % LANES
    if isinstance(amount, int) and amount == 0:
        return x
    return pltpu.roll(x, amount, 1)


def one_hot(cond):
    return jnp.where(cond, 1.0, 0.0).astype(F32)


def exact_dot(a, b):
    return jnp.dot(a, b, precision=lax.Precision.HIGHEST, preferred_element_type=F32)


class Swap:
    def __init__(self, refs, sems, level, place):
        self.ext, self.yf, self.yl, self.yhi, self.ylo, self.px, self.xlo, self.xhi, self.side = refs
        self.send, self.recv = sems
        self.planes, self.rows = FINE[level]
        self.half = 2**level
        self.place = place
        self.copies = []

    def put(self, z, x, packed):
        self.ext[z + 1] = x
        self.yf[z] = x[0:1]
        self.yl[z] = x[self.rows - 1 : self.rows]
        moved = shift_lanes(x, 2 * self.half * z + self.half)
        return jnp.where(lane_of(x.shape) // (2 * self.half) == z, moved, packed)

    def empty(self):
        return jnp.zeros(self.px.shape, F32)

    def start(self, packed):
        self.px[...] = packed
        n = self.planes
        at, size = self.place
        moves = (
            ("gz", 1, self.ext.at[n], self.ext.at[0]),
            ("gz", -1, self.ext.at[1], self.ext.at[n + 1]),
            ("gx", 1, self.yl, self.ylo),
            ("gx", -1, self.yf, self.yhi),
            ("gy", 1, self.px, self.xlo),
            ("gy", -1, self.px, self.xhi),
        )
        for i, (axis, step, src, dst) in enumerate(moves):
            to = tuple(
                lax.rem(at[a] + step + size[a], size[a]) if a == axis else at[a] for a in AXES
            )
            copy = pltpu.make_async_remote_copy(
                src_ref=src,
                dst_ref=dst,
                send_sem=self.send.at[i],
                recv_sem=self.recv.at[i],
                device_id=to,
                device_id_type=MESH,
            )
            copy.start()
            self.copies.append(copy)

    def finish(self):
        at, size = self.place
        for copy in self.copies:
            copy.wait()
        n = self.planes
        self.ext[0] = jnp.where(at["gz"] > 0, self.ext[0], 0.0)
        self.ext[n + 1] = jnp.where(at["gz"] < size["gz"] - 1, self.ext[n + 1], 0.0)
        self.ylo[...] = jnp.where(at["gx"] > 0, self.ylo[...], 0.0)
        self.yhi[...] = jnp.where(at["gx"] < size["gx"] - 1, self.yhi[...], 0.0)
        low = jnp.where(at["gy"] > 0, self.xlo[...], 0.0)
        high = jnp.where(at["gy"] < size["gy"] - 1, self.xhi[...], 0.0)
        self.side[...] = jnp.where(lane_of(low.shape) % (2 * self.half) < self.half, low, high)

    def around(self, z):
        x = self.ext[z + 1]
        row, lane = row_of(x.shape), lane_of(x.shape)
        tall, half = x.shape[0], self.half
        side = shift_lanes(self.side[...], -(2 * half * z + half))
        return x, (
            self.ext[z],
            self.ext[z + 2],
            jnp.where(row == 0, self.ylo[z], pltpu.roll(x, 1, 0)),
            jnp.where(row == self.rows - 1, self.yhi[z], pltpu.roll(x, tall - 1, 0)),
            shift_lanes(jnp.where(lane >= LANES - half, side, x), half),
            shift_lanes(jnp.where(lane < half, side, x), -half),
        )


class Whole:
    def __init__(self, ext, shape):
        self.ext = ext
        self.planes, self.rows, self.half = shape
        self.ext[0] = jnp.zeros(self.ext.shape[1:], F32)
        self.ext[self.planes + 1] = jnp.zeros(self.ext.shape[1:], F32)

    def put(self, z, x, packed):
        self.ext[z + 1] = x
        return packed

    def around(self, z):
        return beside(self.ext[z], self.ext[z + 1], self.ext[z + 2], self.rows, self.half)


def beside(before, x, after, rows, half):
    row, lane = row_of(x.shape), lane_of(x.shape)
    return x, (
        before,
        after,
        jnp.where(row == 0, 0.0, pltpu.roll(x, 1, 0)),
        jnp.where(row == rows - 1, 0.0, pltpu.roll(x, x.shape[0] - 1, 0)),
        shift_lanes(jnp.where(lane >= LANES - half, 0.0, x), half),
        shift_lanes(jnp.where(lane < half, 0.0, x), -half),
    )


def applied(around, faces, z):
    x, near = around
    total = faces[0, z] * (x - near[0])
    for q in range(1, 6):
        total = total + faces[q, z] * (x - near[q])
    return total


def face_weights(field, faces, rate, level):
    scale = 0.5 * 0.25**level

    def body(z, carry):
        x, near = field.around(z)
        diagonal = jnp.zeros_like(x)
        for q in range(6):
            weight = scale * (x + near[q])
            faces[q, z] = weight
            diagonal = diagonal + weight
        inside = diagonal > 0.0
        rate[z] = jnp.where(inside, OMEGA / jnp.where(inside, diagonal, 1.0), 0.0)
        return carry

    loop(field.planes, body, 0)


def pair_down(total, rows, half, scratch):
    scratch[...] = total
    count = total.shape[0] // 2
    both = scratch[pl.ds(0, count, stride=2), :] + scratch[pl.ds(1, count, stride=2), :]
    lane = lane_of(both.shape)
    other = jnp.where(lane // half % 2 == 0, shift_lanes(both, -half), shift_lanes(both, half))
    return 0.125 * (both + other)


def spread(coarse, rows, scratch):
    count = scratch.shape[0] // 2
    scratch[pl.ds(0, count, stride=2), :] = coarse[0:count]
    scratch[pl.ds(1, count, stride=2), :] = coarse[0:count]
    return scratch[...]


def store_layer(dst, z, layer):
    dst[z, 0 : layer.shape[0]] = layer


def down(field, source, faces, level_half, target, scratch):
    def body(z, carry):
        total = None
        for part in range(2):
            i = 2 * z + part
            defect = source[i] - applied(field.around(i), faces, i)
            total = defect if total is None else total + defect
        store_layer(target, z, pair_down(total, field.rows, level_half, scratch))
        return carry

    loop(field.planes // 2, body, 0)


def first_relax(field, source, rate, packed):
    def body(z, carry):
        return field.put(z, rate[z] * source[z], carry)

    return loop(field.planes, body, packed)


def add_coarse(field, old, coarse_layer, packed, scratch):
    def body(z, carry):
        wide = spread(coarse_layer(z), field.rows, scratch)
        for part in range(2):
            i = 2 * z + part
            carry = field.put(i, old.ext[i + 1] + wide, carry)
        return carry

    return loop(field.planes // 2, body, packed)


def relax_into(field, source, faces, rate, put, carry):
    def body(z, carry):
        around = field.around(z)
        return put(z, around[0] + rate[z] * (source[z] - applied(around, faces, z)), carry)

    return loop(field.planes, body, carry)


def restrict_weights(layer, planes, rows, half, target, scratch):
    def body(z, carry):
        store_layer(target, z, pair_down(layer(2 * z) + layer(2 * z + 1), rows, half, scratch))
        return carry

    loop(planes // 2, body, 0)


def kernel(size, names, source_ref, weight_ref, out_ref, residual_ref, *scratch):
    ref = dict(zip(names, scratch))
    at = {a: lax.axis_index(a) for a in AXES}
    place = (at, size)

    def along(axis, step):
        return tuple(lax.rem(at[a] + step, size[a]) if a == axis else at[a] for a in AXES)

    barrier = pltpu.get_barrier_semaphore()
    peers = [(a, k) for a in AXES for k in range(1, size[a])]
    for axis, step in peers:
        pl.semaphore_signal(barrier, inc=1, device_id=along(axis, step), device_id_type=MESH)

    swaps = {}
    for k, name in enumerate(SWAP_FIELDS):
        parts = ("ext", "yf", "yl", "yhi", "ylo", "px", "xlo", "xhi", "side")
        swaps[name] = Swap(
            tuple(ref[f"{name}_{part}"] for part in parts),
            (ref["send"].at[k], ref["recv"].at[k]),
            int(name[1]),
            place,
        )

    for level in range(4):
        planes, rows = FINE[level]
        if level > 0:
            ref[f"s{level}"][...] = jnp.zeros(ref[f"s{level}"].shape, F32)
            ref[f"k{level}"][...] = jnp.zeros(ref[f"k{level}"].shape, F32)
            below = weight_ref if level == 1 else ref[f"k{level - 1}"]
            restrict_weights(
                lambda z, below=below: below[z],
                2 * planes,
                2 * rows,
                2 ** (level - 1),
                ref[f"k{level}"],
                ref[f"t{level - 1}"],
            )
    ref["s4"][...] = jnp.zeros(ref["s4"].shape, F32)
    ref["k4"][...] = jnp.zeros(ref["k4"].shape, F32)
    restrict_weights(lambda z: ref["k3"][z], 2, 4, 8, ref["k4"], ref["t3"])
    packed = {}
    for level in range(4):
        swap = swaps[f"w{level}"]
        below = weight_ref if level == 0 else ref[f"k{level}"]
        packed[level] = loop(
            swap.planes,
            lambda z, c, swap=swap, below=below: swap.put(z, below[z], c),
            swap.empty(),
        )
    pl.semaphore_wait(barrier, len(peers))
    for level in range(4):
        swaps[f"w{level}"].start(packed[level])
    for level in range(4):
        swap = swaps[f"w{level}"]
        swap.finish()
        face_weights(swap, ref[f"f{level}"], ref[f"d{level}"], level)

    sources = [source_ref, ref["s1"], ref["s2"], ref["s3"], ref["s4"]]
    for level in range(4):
        swap = swaps[f"v{level}"]
        swap.start(first_relax(swap, sources[level], ref[f"d{level}"], swap.empty()))
        swap.finish()
        down(swap, sources[level], ref[f"f{level}"], 2**level, sources[level + 1], ref[f"t{level}"])

    tile = (8, LANES)
    lane, row = lane_of(tile), row_of(tile)
    own = jnp.concatenate([ref["s4"][0][0:2], ref["k4"][0][0:2], jnp.zeros((4, LANES), F32)], 0)
    square = (LANES, LANES)
    pick = one_hot(row_of(square) == lane_of(square) % 8 * 16)
    shrunk = exact_dot(own, pick)
    line = jnp.sum(jnp.where(lane // 32 == row, shrunk, 0.0), axis=0, keepdims=True)
    ref["g0"][...] = line

    def all_to_all(axis, src, dst, send, recv):
        copies = []
        for step in range(1, size[axis]):
            copy = pltpu.make_async_remote_copy(
                src_ref=src,
                dst_ref=dst.at[at[axis]],
                send_sem=send.at[step],
                recv_sem=recv.at[step],
                device_id=along(axis, step),
                device_id_type=MESH,
            )
            copy.start()
            copies.append(copy)
        dst[at[axis]] = src[...]
        for copy in copies:
            copy.wait()

    all_to_all("gy", ref["g0"], ref["g1"], ref["send_gy"], ref["recv_gy"])
    lane1 = lane_of((1, LANES))
    merged = jnp.zeros((1, LANES), F32)
    for k in range(size["gy"]):
        merged = jnp.where(lane1 // 8 % 4 == k, ref["g1"][k], merged)
    ref["g2"][...] = merged
    all_to_all("gz", ref["g2"], ref["g3"], ref["send_gz"], ref["recv_gz"])
    all_to_all("gx", ref["g3"], ref["g4"], ref["send_gx"], ref["recv_gx"])

    wide = (LANES, 4 * LANES)
    expand = one_hot(row_of(wide) == lane_of(wide) // LANES * 32 + lane_of(wide) % LANES // 4)
    for z in range(size["gz"]):
        for k in range(size["gx"]):
            ref["g5"][8 * z + k : 8 * z + k + 1, :] = ref["g4"][k, z]
    ref["g6"][...] = exact_dot(ref["g5"][...], expand)
    fields = {}
    for level in range(4, 7):
        for kind in "wvc":
            fields[kind, level] = Whole(ref[f"{kind}{level}_ext"], COARSE[level - 4])
    for z in range(16):
        block = ref["g6"][8 * z : 8 * z + 8, :]
        for part in range(2):
            rows = pl.ds(part, 8, stride=2)
            ref["q4"][z, rows, :] = block[:, part * LANES : (part + 1) * LANES]
            ref["w4_ext"][z + 1, rows, :] = block[:, (part + 2) * LANES : (part + 3) * LANES]

    for level in (4, 5):
        planes, rows, half = COARSE[level - 4]
        field = fields["w", level]
        if level == 5:
            ref["k6"][...] = jnp.zeros(ref["k6"].shape, F32)
            ref["q6"][...] = jnp.zeros(ref["q6"].shape, F32)
        target = ref[f"k{level + 1}"]
        restrict_weights(
            lambda z, field=field: field.ext[z + 1], planes, rows, half, target, ref[f"t{level}"]
        )
        for z in range(planes // 2):
            fields["w", level + 1].put(z, target[z], 0)
    for level in (4, 5, 6):
        face_weights(fields["w", level], ref[f"f{level}"], ref[f"d{level}"], level)
    for level in (4, 5):
        field, faces = fields["v", level], ref[f"f{level}"]
        first_relax(field, ref[f"q{level}"], ref[f"d{level}"], 0)
        down(field, ref[f"q{level}"], faces, field.half, ref[f"q{level + 1}"], ref[f"t{level}"])

    planes, rows, half = COARSE[2]
    faces, rate, source = ref["f6"], ref["d6"], ref["q6"]
    zero = jnp.zeros((8, LANES), F32)

    def sweep(_, value):
        out = []
        for z in range(planes):
            before = value[z - 1] if z > 0 else zero
            after = value[z + 1] if z < planes - 1 else zero
            around = beside(before, value[z], after, rows, half)
            out.append(value[z] + rate[z] * (source[z] - applied(around, faces, z)))
        return tuple(out)

    start = tuple(rate[z] * source[z] for z in range(planes))
    bottom = lax.fori_loop(0, 7, sweep, start)
    for z in range(planes):
        ref["e6"][z] = bottom[z]
    for level in (5, 4):
        field = fields["c", level]
        coarse = ref[f"e{level + 1}"]
        add_coarse(
            field, fields["v", level], lambda z, c=coarse: c[z], 0, ref[f"t{level}"]
        )
        target = ref[f"e{level}"]

        def put(z, x, carry, target=target):
            target[z] = x
            return carry

        relax_into(field, ref[f"q{level}"], ref[f"f{level}"], ref[f"d{level}"], put, 0)

    pick_lane = one_hot(row_of(square) == (8 * at["gy"] + lane_of(square) // 16) * 4)
    pick_row = one_hot(lane_of((8, 16)) == 2 * at["gx"] + row_of((8, 16)))
    mine = exact_dot(pick_row, exact_dot(ref["e4"][at["gz"]], pick_lane))
    ref["e_own"][...] = mine

    coarse_layer = lambda z: ref["e_own"][...]
    for level in (3, 2, 1, 0):
        swap = swaps[f"c{level}"]
        old = swaps[f"v{level}"]
        swap.start(add_coarse(swap, old, coarse_layer, swap.empty(), ref[f"t{level}"]))
        swap.finish()
        source, faces, rate = sources[level], ref[f"f{level}"], ref[f"d{level}"]
        if level > 0:
            target = ref[f"e{level}"]

            def put(z, x, carry, target=target):
                target[z] = x
                return carry

            relax_into(swap, source, faces, rate, put, 0)
            coarse_layer = lambda z, target=target: target[z]
        else:
            last = swaps["r0"]

            def put(z, x, carry):
                out_ref[z] = x
                return last.put(z, x, carry)

            last.start(relax_into(swap, source, faces, rate, put, last.empty()))
            last.finish()

            def body(z, carry):
                residual_ref[z] = source[z] - applied(last.around(z), faces, z)
                return carry

            loop(16, body, 0)


def buffers(size):
    shapes = {}

    def vmem(name, *shape):
        shapes[name] = pltpu.VMEM(shape, F32)

    for name in SWAP_FIELDS:
        planes, rows = FINE[int(name[1])]
        tall = padded_rows(rows)
        vmem(f"{name}_ext", planes + 2, tall, LANES)
        for part in ("yf", "yl", "yhi", "ylo"):
            vmem(f"{name}_{part}", planes, 1, LANES)
        for part in ("px", "xlo", "xhi", "side"):
            vmem(f"{name}_{part}", tall, LANES)
    for level, (planes, rows) in enumerate(FINE):
        tall = padded_rows(rows)
        vmem(f"f{level}", 6, planes, tall, LANES)
        vmem(f"d{level}", planes, tall, LANES)
        vmem(f"t{level}", tall, LANES)
        if level > 0:
            vmem(f"s{level}", planes, tall, LANES)
            vmem(f"k{level}", planes, tall, LANES)
            vmem(f"e{level}", planes, tall, LANES)
    vmem("s4", 1, 8, LANES)
    vmem("k4", 1, 8, LANES)
    vmem("e_own", 8, LANES)
    for level, (planes, rows, _) in zip((4, 5, 6), COARSE):
        tall = padded_rows(rows)
        for kind in "wvc":
            vmem(f"{kind}{level}_ext", planes + 2, tall, LANES)
        vmem(f"f{level}", 6, planes, tall, LANES)
        vmem(f"d{level}", planes, tall, LANES)
        vmem(f"q{level}", planes, tall, LANES)
        vmem(f"e{level}", planes, tall, LANES)
        vmem(f"t{level}", tall, LANES)
        if level > 4:
            vmem(f"k{level}", planes, tall, LANES)
    vmem("g0", 1, LANES)
    vmem("g1", size["gy"], 1, LANES)
    vmem("g2", 1, LANES)
    vmem("g3", size["gz"], 1, LANES)
    vmem("g4", size["gx"], size["gz"], 1, LANES)
    vmem("g5", size["gx"] * size["gz"], LANES)
    vmem("g6", size["gx"] * size["gz"], 4 * LANES)
    shapes["send"] = pltpu.SemaphoreType.DMA((len(SWAP_FIELDS), 6))
    shapes["recv"] = pltpu.SemaphoreType.DMA((len(SWAP_FIELDS), 6))
    for axis in AXES:
        shapes[f"send_{axis}"] = pltpu.SemaphoreType.DMA((size[axis],))
        shapes[f"recv_{axis}"] = pltpu.SemaphoreType.DMA((size[axis],))
    return shapes


def solution(mesh):
    size = dict(mesh.shape)
    spec = P("gz", "gx", "gy")

    def body(source, conductivity):
        shapes = buffers(size)
        block = jax.ShapeDtypeStruct(source.shape, F32)

        def run(*refs):
            kernel(size, tuple(shapes), *refs)

        return pl.pallas_call(
            run,
            out_shape=(block, block),
            in_specs=[pl.BlockSpec(memory_space=pltpu.VMEM)] * 2,
            out_specs=[pl.BlockSpec(memory_space=pltpu.VMEM)] * 2,
            scratch_shapes=list(shapes.values()),
            compiler_params=pltpu.CompilerParams(
                collective_id=0, has_side_effects=True, vmem_limit_bytes=48 * 1024 * 1024
            ),
        )(source, conductivity)

    return jax.shard_map(
        body, mesh=mesh, in_specs=(spec, spec), out_specs=(spec, spec), check_vma=False
    )
```

```python
import jax
import jax.numpy as jnp
from jax import lax
from jax.experimental import pallas as pl
from jax.experimental.pallas import tpu as pltpu
from jax.sharding import PartitionSpec as P

MESH = pl.DeviceIdType.MESH
AXES = ("gx", "gy", "gz")
OMEGA = 2.0 / 3.0
LANES = 128
F32 = jnp.float32

FINE = ((16, 32),)
RING = {1: (24, 32, 1), 2: (12, 16, 2), 3: (6, 8, 4)}
MARGIN = 8
COARSE = ((16, 16, 4), (8, 8, 8), (4, 4, 16))
SWAP_FIELDS = ("w0", "v0", "c0", "r0")
SIDES = tuple((a, b, c) for a in (-1, 0, 1) for b in (-1, 0, 1) for c in (-1, 0, 1) if (a, b, c) != (0, 0, 0))


def padded_rows(rows):
    return max(rows, 8)


def lane_of(shape):
    return lax.broadcasted_iota(jnp.int32, shape, len(shape) - 1)


def row_of(shape):
    return lax.broadcasted_iota(jnp.int32, shape, len(shape) - 2)


def loop(count, body, carry):
    if count <= 4:
        for i in range(count):
            carry = body(i, carry)
        return carry
    return lax.fori_loop(0, count, body, carry, unroll=2)


def shift_lanes(x, amount):
    amount = lax.rem(amount + LANES, LANES) if not isinstance(amount, int) else amount % LANES
    if isinstance(amount, int) and amount == 0:
        return x
    return pltpu.roll(x, amount, 1)


def one_hot(cond):
    return jnp.where(cond, 1.0, 0.0).astype(F32)


def exact_dot(a, b):
    return jnp.dot(a, b, precision=lax.Precision.HIGHEST, preferred_element_type=F32)


class Swap:
    def __init__(self, refs, sems, level, place):
        self.ext, self.yf, self.yl, self.yhi, self.ylo, self.px, self.xlo, self.xhi, self.side = refs
        self.send, self.recv = sems
        self.planes, self.rows = FINE[level]
        self.half = 2**level
        self.place = place
        self.copies = []

    def put(self, z, x, packed):
        self.ext[z + 1] = x
        self.yf[z] = x[0:1]
        self.yl[z] = x[self.rows - 1 : self.rows]
        moved = shift_lanes(x, 2 * self.half * z + self.half)
        return jnp.where(lane_of(x.shape) // (2 * self.half) == z, moved, packed)

    def empty(self):
        return jnp.zeros(self.px.shape, F32)

    def start(self, packed):
        self.px[...] = packed
        n = self.planes
        at, size = self.place
        moves = (
            ("gz", 1, self.ext.at[n], self.ext.at[0]),
            ("gz", -1, self.ext.at[1], self.ext.at[n + 1]),
            ("gx", 1, self.yl, self.ylo),
            ("gx", -1, self.yf, self.yhi),
            ("gy", 1, self.px, self.xlo),
            ("gy", -1, self.px, self.xhi),
        )
        for i, (axis, step, src, dst) in enumerate(moves):
            to = tuple(
                lax.rem(at[a] + step + size[a], size[a]) if a == axis else at[a] for a in AXES
            )
            copy = pltpu.make_async_remote_copy(
                src_ref=src,
                dst_ref=dst,
                send_sem=self.send.at[i],
                recv_sem=self.recv.at[i],
                device_id=to,
                device_id_type=MESH,
            )
            copy.start()
            self.copies.append(copy)

    def finish(self):
        at, size = self.place
        for copy in self.copies:
            copy.wait()
        n = self.planes
        self.ext[0] = jnp.where(at["gz"] > 0, self.ext[0], 0.0)
        self.ext[n + 1] = jnp.where(at["gz"] < size["gz"] - 1, self.ext[n + 1], 0.0)
        self.ylo[...] = jnp.where(at["gx"] > 0, self.ylo[...], 0.0)
        self.yhi[...] = jnp.where(at["gx"] < size["gx"] - 1, self.yhi[...], 0.0)
        low = jnp.where(at["gy"] > 0, self.xlo[...], 0.0)
        high = jnp.where(at["gy"] < size["gy"] - 1, self.xhi[...], 0.0)
        self.side[...] = jnp.where(lane_of(low.shape) % (2 * self.half) < self.half, low, high)

    def around(self, z):
        x = self.ext[z + 1]
        row, lane = row_of(x.shape), lane_of(x.shape)
        tall, half = x.shape[0], self.half
        side = shift_lanes(self.side[...], -(2 * half * z + half))
        return x, (
            self.ext[z],
            self.ext[z + 2],
            jnp.where(row == 0, self.ylo[z], pltpu.roll(x, 1, 0)),
            jnp.where(row == self.rows - 1, self.yhi[z], pltpu.roll(x, tall - 1, 0)),
            shift_lanes(jnp.where(lane >= LANES - half, side, x), half),
            shift_lanes(jnp.where(lane < half, side, x), -half),
        )


class Ring:
    def __init__(self, ext, level):
        self.ext = ext
        self.planes, self.rows, self.half = RING[level]

    def put(self, z, x, carry):
        self.ext[z] = x
        return carry

    def around(self, z):
        n = self.planes
        if isinstance(z, int):
            before, after = (z + n - 1) % n, (z + 1) % n
        else:
            before, after = lax.rem(z + n - 1, n), lax.rem(z + 1, n)
        x = self.ext[z]
        return x, (
            self.ext[before],
            self.ext[after],
            pltpu.roll(x, 1, 0),
            pltpu.roll(x, x.shape[0] - 1, 0),
            shift_lanes(x, self.half),
            shift_lanes(x, -self.half),
        )


def ring_loop(first, count, total, body):
    def step(i, carry):
        z = first + i
        body(z % total if isinstance(z, int) else lax.rem(z, total))
        return carry

    loop(count, step, 0)


class Margin:
    def __init__(self, ext, px, left, right, sems, place):
        self.ext, self.px, self.left, self.right = ext, px, left, right
        self.send, self.recv = sems
        self.place = place
        self.copies = []

    def start(self):
        lane = lane_of((16, LANES))
        packed = jnp.zeros((16, LANES), F32)
        for z in range(MARGIN):
            x = self.ext[z, 0:16]
            spot = lane // 16 == z
            packed = jnp.where(spot & (lane % 16 < 8), shift_lanes(x, 16 * z - 64), packed)
            packed = jnp.where(spot & (lane % 16 >= 8), shift_lanes(x, 16 * z), packed)
        self.px[...] = packed
        at, size = self.place
        rows_out = {-1: pl.ds(0, 8), 0: pl.ds(0, 16), 1: pl.ds(8, 8)}
        rows_in = {-1: pl.ds(16, 8), 0: pl.ds(0, 16), 1: pl.ds(24, 8)}
        planes_in = {-1: pl.ds(8, 8), 0: pl.ds(0, 8), 1: pl.ds(16, 8)}
        block_in = {-1: 1, 0: 0, 1: 2}
        order = sorted(range(26), key=lambda i: sum(map(abs, SIDES[i])))
        for i in order:
            dz, dx, dy = SIDES[i]
            if dy == 0:
                src = self.ext.at[pl.ds(0, 8), rows_out[dx], :]
                dst = self.ext.at[planes_in[dz], rows_in[dx], :]
            else:
                land = self.left if dy == 1 else self.right
                src = self.px.at[rows_out[dx], :]
                dst = land.at[block_in[dz], rows_in[dx], :]
            copy = pltpu.make_async_remote_copy(
                src_ref=src,
                dst_ref=dst,
                send_sem=self.send.at[i],
                recv_sem=self.recv.at[i],
                device_id=neighbour(self.place, dz, dx, dy),
                device_id_type=MESH,
            )
            copy.start()
            self.copies.append(copy)

    def finish(self):
        at, size = self.place
        for copy in self.copies:
            copy.wait()
        shape = (32, LANES)
        row, lane = row_of(shape), lane_of(shape)
        for block in range(3):
            z_ok = (True, at["gz"] < size["gz"] - 1, at["gz"] > 0)[block]
            ok = (row < 16) | ((row < 24) & (at["gx"] < size["gx"] - 1)) | ((row >= 24) & (at["gx"] > 0))
            if block > 0:
                ok = ok & z_ok
            low = ok & (lane < 8) & (at["gy"] > 0)
            high = ok & (lane >= 72) & (lane < 80) & (at["gy"] < size["gy"] - 1)
            own = ok & (lane >= 8) & (lane < 72)
            sides = jnp.where(lane % 16 < 8, self.left[block], self.right[block])
            self.left[block] = sides

            def body(i, carry, block=block, low=low, high=high, own=own):
                z = 8 * block + i
                sides = self.left[block]
                merged = jnp.where(own, self.ext[z], 0.0)
                merged = jnp.where(low, shift_lanes(sides, -16 * i), merged)
                merged = jnp.where(high, shift_lanes(sides, 64 - 16 * i), merged)
                self.ext[z] = merged
                return carry

            loop(8, body, 0)


def neighbour(place, dz, dx, dy):
    at, size = place
    step = {"gz": dz, "gx": dx, "gy": dy}
    return tuple(lax.rem(at[a] + step[a] + size[a], size[a]) if step[a] else at[a] for a in AXES)


class Whole:
    def __init__(self, ext, shape):
        self.ext = ext
        self.planes, self.rows, self.half = shape
        self.ext[0] = jnp.zeros(self.ext.shape[1:], F32)
        self.ext[self.planes + 1] = jnp.zeros(self.ext.shape[1:], F32)

    def put(self, z, x, packed):
        self.ext[z + 1] = x
        return packed

    def around(self, z):
        return beside(self.ext[z], self.ext[z + 1], self.ext[z + 2], self.rows, self.half)


def beside(before, x, after, rows, half):
    row, lane = row_of(x.shape), lane_of(x.shape)
    return x, (
        before,
        after,
        jnp.where(row == 0, 0.0, pltpu.roll(x, 1, 0)),
        jnp.where(row == rows - 1, 0.0, pltpu.roll(x, x.shape[0] - 1, 0)),
        shift_lanes(jnp.where(lane >= LANES - half, 0.0, x), half),
        shift_lanes(jnp.where(lane < half, 0.0, x), -half),
    )


def applied(around, faces, z):
    x, near = around
    total = faces[0, z] * (x - near[0])
    for q in range(1, 6):
        total = total + faces[q, z] * (x - near[q])
    return total


def face_weights(field, faces, rate, level):
    scale = 0.5 * 0.25**level

    def body(z, carry):
        x, near = field.around(z)
        diagonal = jnp.zeros_like(x)
        for q in range(6):
            weight = scale * (x + near[q])
            faces[q, z] = weight
            diagonal = diagonal + weight
        inside = x > 0.0
        rate[z] = jnp.where(inside, OMEGA / jnp.where(inside, diagonal, 1.0), 0.0)
        return carry

    loop(field.planes, body, 0)


def pair_down(total, rows, half, scratch):
    scratch[...] = total
    count = total.shape[0] // 2
    both = scratch[pl.ds(0, count, stride=2), :] + scratch[pl.ds(1, count, stride=2), :]
    lane = lane_of(both.shape)
    other = jnp.where(lane // half % 2 == 0, shift_lanes(both, -half), shift_lanes(both, half))
    return 0.125 * (both + other)


def spread(coarse, rows, scratch):
    count = scratch.shape[0] // 2
    scratch[pl.ds(0, count, stride=2), :] = coarse[0:count]
    scratch[pl.ds(1, count, stride=2), :] = coarse[0:count]
    return scratch[...]


def store_layer(dst, z, layer):
    dst[z, 0 : layer.shape[0]] = layer


def down(field, source, faces, level_half, target, scratch):
    def body(z, carry):
        total = None
        for part in range(2):
            i = 2 * z + part
            defect = source[i] - applied(field.around(i), faces, i)
            total = defect if total is None else total + defect
        store_layer(target, z, pair_down(total, field.rows, level_half, scratch))
        return carry

    loop(field.planes // 2, body, 0)


def first_relax(field, source, rate, packed):
    def body(z, carry):
        return field.put(z, rate[z] * source[z], carry)

    return loop(field.planes, body, packed)


def add_coarse(field, old, coarse_layer, packed, scratch):
    def body(z, carry):
        wide = spread(coarse_layer(z), field.rows, scratch)
        for part in range(2):
            i = 2 * z + part
            carry = field.put(i, old.ext[i + 1] + wide, carry)
        return carry

    return loop(field.planes // 2, body, packed)


def relax_into(field, source, faces, rate, put, carry):
    def body(z, carry):
        around = field.around(z)
        return put(z, around[0] + rate[z] * (source[z] - applied(around, faces, z)), carry)

    return loop(field.planes, body, carry)


def restrict_weights(layer, planes, rows, half, target, scratch):
    def body(z, carry):
        store_layer(target, z, pair_down(layer(2 * z) + layer(2 * z + 1), rows, half, scratch))
        return carry

    loop(planes // 2, body, 0)


def kernel(size, names, source_ref, weight_ref, out_ref, residual_ref, *scratch):
    ref = dict(zip(names, scratch))
    at = {a: lax.axis_index(a) for a in AXES}
    place = (at, size)

    peers = set()
    for dz, dx, dy in SIDES:
        peers.add((dz % size["gz"], dx % size["gx"], dy % size["gy"]))
    peers.update((k, 0, 0) for k in range(1, size["gz"]))
    flat = [(i, j) for i in range(size["gx"]) for j in range(size["gy"]) if (i, j) != (0, 0)]
    peers.update((0, i, j) for i, j in flat)
    barrier = pltpu.get_barrier_semaphore()
    for step in sorted(peers):
        pl.semaphore_signal(
            barrier, inc=1, device_id=neighbour(place, *step), device_id_type=MESH
        )

    swaps = {}
    for k, name in enumerate(SWAP_FIELDS):
        parts = ("ext", "yf", "yl", "yhi", "ylo", "px", "xlo", "xhi", "side")
        swaps[name] = Swap(
            tuple(ref[f"{name}_{part}"] for part in parts),
            (ref["send"].at[k], ref["recv"].at[k]),
            int(name[1]),
            place,
        )
    margins = {}
    for k, name in enumerate(("w1", "s1")):
        margins[name] = Margin(
            *(ref[f"{name}{part}"] for part in ("", "_px", "_left", "_right")),
            (ref["send_side"].at[k], ref["recv_side"].at[k]),
            place,
        )
    square = (LANES, LANES)
    to_ring = one_hot(row_of(square) == 2 * (lane_of(square) - MARGIN))

    def into_ring(two_lanes, ring):
        packed = exact_dot(two_lanes[...].reshape(LANES, LANES), to_ring)
        ring[0:8, 0:16] = packed.reshape(8, 16, LANES)

    swap = swaps["w0"]
    packed = loop(16, lambda z, c: swap.put(z, weight_ref[z], c), swap.empty())
    pl.semaphore_wait(barrier, len(peers))
    swap.start(packed)
    restrict_weights(lambda z: weight_ref[z], 16, 32, 1, ref["k1"], ref["t0"])
    into_ring(ref["k1"], ref["w1"])
    margins["w1"].start()
    swap.finish()
    face_weights(swap, ref["f0"], ref["d0"], 0)
    swap = swaps["v0"]
    swap.start(first_relax(swap, source_ref, ref["d0"], swap.empty()))

    margins["w1"].finish()
    rings = {}
    for level in (1, 2, 3):
        for kind in "wvc":
            rings[kind, level] = Ring(ref[f"{kind}{level}"], level)
        field = rings["w", level]
        face_weights(field, ref[f"f{level}"], ref[f"d{level}"], level)
        target = ref[f"w{level + 1}"] if level < 3 else ref["k4"]
        planes = field.planes if level < 3 else 2
        restrict_weights(
            lambda z, field=field: field.ext[z], planes, field.rows, field.half, target, ref[f"t{level}"]
        )
    swap.finish()
    down(swap, source_ref, ref["f0"], 1, ref["k1"], ref["t0"])
    into_ring(ref["k1"], ref["s1"])
    margins["s1"].start()
    margins["s1"].finish()

    spans = {1: ((0, 24), (9, 10)), 2: ((9, 10), (5, 4)), 3: ((5, 4), (0, 1))}
    for level in (1, 2, 3):
        field, faces, rate = rings["v", level], ref[f"f{level}"], ref[f"d{level}"]
        source = ref[f"s{level}"]
        (first, count), (low, pairs) = spans[level]

        def relax_plane(z, field=field, rate=rate, source=source):
            field.put(z, rate[z] * source[z], 0)

        ring_loop(first, count, field.planes, relax_plane)

        def pair(z, field=field, faces=faces, source=source, level=level):
            total = None
            for part in range(2):
                i = 2 * z + part
                defect = source[i] - applied(field.around(i), faces, i)
                total = defect if total is None else total + defect
            below = pair_down(total, field.rows, field.half, ref[f"t{level}"])
            store_layer(ref[f"s{level + 1}"], z, below)

        ring_loop(low, pairs, field.planes // 2, pair)

    tile = (8, LANES)
    lane, row = lane_of(tile), row_of(tile)
    own = jnp.concatenate([ref["s4"][0][0:2], ref["k4"][0][0:2], jnp.zeros((4, LANES), F32)], 0)
    pick = one_hot(row_of(square) == MARGIN + lane_of(square) % 8 * 8)
    shrunk = exact_dot(own, pick)
    line = jnp.sum(jnp.where(lane // 32 == row, shrunk, 0.0), axis=0, keepdims=True)
    ref["g0"][...] = line

    copies = []

    def send(src, dst, key, i, step):
        copy = pltpu.make_async_remote_copy(
            src_ref=src,
            dst_ref=dst,
            send_sem=ref[f"send_{key}"].at[i],
            recv_sem=ref[f"recv_{key}"].at[i],
            device_id=neighbour(place, *step),
            device_id_type=MESH,
        )
        copy.start()
        return copy

    for i, (dx, dy) in enumerate(flat):
        copies.append(send(ref["g0"], ref["g1"].at[at["gy"], at["gx"]], "flat", i, (0, dx, dy)))
    ref["g1"][at["gy"], at["gx"]] = line

    def stacked(name):
        return jnp.where(row < 4, ref[name][0], pltpu.roll(ref[name][1], 4, 0))

    ref["own3"][...] = jnp.where(
        lane < 64, shift_lanes(stacked("s3"), -MARGIN), shift_lanes(stacked("d3"), 64 - MARGIN)
    )
    side_copies = [
        send(ref["own3"], ref["side3"].at[i], "side3", i, SIDES[i]) for i in range(26)
    ]
    for copy in copies:
        copy.wait()
    merged = jnp.zeros(tile, F32)
    for k in range(size["gy"]):
        rows = jnp.concatenate([ref["g1"][k, i] for i in range(size["gx"])], 0)
        merged = jnp.where(lane // 8 % 4 == k, rows, merged)
    ref["g2"][...] = merged
    copies = [
        send(ref["g2"], ref["g5"].at[at["gz"]], "gz", k, (k, 0, 0)) for k in range(1, size["gz"])
    ]
    ref["g5"][at["gz"]] = merged

    for copy in side_copies:
        copy.wait()
    inside = {
        "gz": {0: True, 1: at["gz"] < size["gz"] - 1, -1: at["gz"] > 0},
        "gx": {0: True, 1: at["gx"] < size["gx"] - 1, -1: at["gx"] > 0},
        "gy": {0: True, 1: at["gy"] < size["gy"] - 1, -1: at["gy"] > 0},
    }

    def from_side(dz, dx, dy):
        if (dz, dx, dy) == (0, 0, 0):
            return ref["own3"][...]
        x = ref["side3"][SIDES.index((-dz, -dx, -dy))]
        for axis, step in (("gz", dz), ("gx", dx), ("gy", dy)):
            if step:
                x = jnp.where(inside[axis][step], x, 0.0)
        return x

    for block, dz in enumerate((0, 1, -1)):
        column = {}
        for dy in (-1, 0, 1):
            mid, up, low = (from_side(dz, dx, dy) for dx in (0, 1, -1))
            turn = lambda x: pltpu.roll(x, 4, 0)
            far = jnp.where(row < 6, turn(up), turn(low))
            column[0, dy] = jnp.where(row < 4, mid, far)
            far = jnp.where(row < 6, up, low)
            column[1, dy] = jnp.where(row < 4, turn(mid), far)
        for part in range(2):
            z = 2 * block + part
            mid = column[part, 0]
            for name, base in (("s3", 0), ("d3", 64)):
                ends = jnp.where(
                    lane < 8,
                    shift_lanes(column[part, -1], 72 - base),
                    shift_lanes(column[part, 1], 72 - base),
                )
                body = shift_lanes(mid, MARGIN - base)
                full = jnp.where((lane >= 8) & (lane < 72), body, jnp.where(lane < 80, ends, 0.0))
                ref[name][z] = full
            rings["v", 3].put(z, ref["d3"][z] * ref["s3"][z], 0)
    for copy in copies:
        copy.wait()

    wide = (LANES, 4 * LANES)
    expand = one_hot(row_of(wide) == lane_of(wide) // LANES * 32 + lane_of(wide) % LANES // 4)
    ref["g6"][...] = exact_dot(ref["g5"][...].reshape(LANES, LANES), expand)
    fields = {}
    for level in range(4, 7):
        for kind in "wvc":
            fields[kind, level] = Whole(ref[f"{kind}{level}_ext"], COARSE[level - 4])
    for z in range(16):
        block = ref["g6"][8 * z : 8 * z + 8, :]
        for part in range(2):
            rows = pl.ds(part, 8, stride=2)
            ref["q4"][z, rows, :] = block[:, part * LANES : (part + 1) * LANES]
            ref["w4_ext"][z + 1, rows, :] = block[:, (part + 2) * LANES : (part + 3) * LANES]

    for level in (4, 5):
        planes, rows, half = COARSE[level - 4]
        field = fields["w", level]
        if level == 5:
            ref["k6"][...] = jnp.zeros(ref["k6"].shape, F32)
            ref["q6"][...] = jnp.zeros(ref["q6"].shape, F32)
        target = ref[f"k{level + 1}"]
        restrict_weights(
            lambda z, field=field: field.ext[z + 1], planes, rows, half, target, ref[f"t{level}"]
        )
        for z in range(planes // 2):
            fields["w", level + 1].put(z, target[z], 0)
    for level in (4, 5, 6):
        face_weights(fields["w", level], ref[f"f{level}"], ref[f"d{level}"], level)
    for level in (4, 5):
        field, faces = fields["v", level], ref[f"f{level}"]
        first_relax(field, ref[f"q{level}"], ref[f"d{level}"], 0)
        down(field, ref[f"q{level}"], faces, field.half, ref[f"q{level + 1}"], ref[f"t{level}"])

    planes, rows, half = COARSE[2]
    faces, rate, source = ref["f6"], ref["d6"], ref["q6"]
    zero = jnp.zeros((8, LANES), F32)

    def sweep(_, value):
        out = []
        for z in range(planes):
            before = value[z - 1] if z > 0 else zero
            after = value[z + 1] if z < planes - 1 else zero
            around = beside(before, value[z], after, rows, half)
            out.append(value[z] + rate[z] * (source[z] - applied(around, faces, z)))
        return tuple(out)

    start = tuple(rate[z] * source[z] for z in range(planes))
    bottom = lax.fori_loop(0, 7, sweep, start)
    for z in range(planes):
        ref["e6"][z] = bottom[z]
    for level in (5, 4):
        field = fields["c", level]
        coarse = ref[f"e{level + 1}"]
        add_coarse(
            field, fields["v", level], lambda z, c=coarse: c[z], 0, ref[f"t{level}"]
        )
        target = ref[f"e{level}"]

        def put(z, x, carry, target=target):
            target[z] = x
            return carry

        relax_into(field, ref[f"q{level}"], ref[f"f{level}"], ref[f"d{level}"], put, 0)

    pick_lane = one_hot(row_of(square) == (8 * at["gy"] - 1 + lane_of(square) // 8) * 4)
    coarse_row = (row_of((8, 16)) // 2 + 1) % 4 - 1
    pick_row = one_hot(lane_of((8, 16)) == 2 * at["gx"] + coarse_row)
    for block, dz in enumerate((0, 1, -1)):
        layer = ref["e4"][jnp.clip(at["gz"] + dz, 0, size["gz"] - 1)]
        if dz:
            layer = jnp.where(inside["gz"][dz], layer, 0.0)
        up = exact_dot(pick_row, exact_dot(layer, pick_lane))
        for part in range(2):
            z = 2 * block + part
            rings["c", 3].put(z, rings["v", 3].ext[z] + up, 0)

    for level, first, count in ((3, 5, 4), (2, 11, 6), (1, 23, 10)):
        field, faces, rate = rings["c", level], ref[f"f{level}"], ref[f"d{level}"]
        source, target = ref[f"s{level}"], ref[f"e{level}"]
        if level < 3:
            coarse, scratch = ref[f"e{level + 1}"], ref[f"t{level}"]

            def lift(z, field=field, coarse=coarse, scratch=scratch, level=level):
                wide = spread(coarse[z], field.rows, scratch)
                for part in range(2):
                    i = 2 * z + part
                    field.put(i, rings["v", level].ext[i] + wide, 0)

            ring_loop(first // 2, (count + 2) // 2, field.planes // 2, lift)

        def relax_plane(z, field=field, faces=faces, rate=rate, source=source, target=target):
            around = field.around(z)
            target[z] = around[0] + rate[z] * (source[z] - applied(around, faces, z))

        ring_loop(first, count, field.planes, relax_plane)

    to_fine = one_hot(row_of(square) == MARGIN + lane_of(square) // 2)
    swap, old = swaps["c0"], swaps["v0"]
    scratch = ref["t1w"]
    side = old.side[...]

    def lifted(zc):
        return spread(exact_dot(ref["e1"][zc], to_fine), 0, scratch)

    def lift(zc, side):
        layer = ref["e1"][zc]
        wide = spread(exact_dot(layer, to_fine), 0, scratch)
        at_lane = lane_of(square) // 4 == zc
        ends = one_hot(
            at_lane
            & (row_of(square) == jnp.where(lane_of(square) % 2 == 0, MARGIN - 1, MARGIN + 64))
        )
        side = side + spread(exact_dot(layer, ends), 0, scratch)[0:32]
        for part in range(2):
            i = 2 * zc + part
            swap.ext[i + 1] = old.ext[i + 1] + wide[0:32]
            swap.yhi[i] = old.yhi[i] + jnp.where(inside["gx"][1], wide[32:33], 0.0)
            swap.ylo[i] = old.ylo[i] + jnp.where(inside["gx"][-1], wide[63:64], 0.0)
        return side

    swap.side[...] = loop(8, lift, side)
    swap.ext[17] = old.ext[17] + lifted(8)[0:32]
    swap.ext[0] = old.ext[0] + lifted(23)[0:32]
    last = swaps["r0"]
    faces, rate = ref["f0"], ref["d0"]

    def put(z, x, carry):
        out_ref[z] = x
        return last.put(z, x, carry)

    last.start(relax_into(swap, source_ref, faces, rate, put, last.empty()))
    last.finish()

    def body(z, carry):
        residual_ref[z] = source_ref[z] - applied(last.around(z), faces, z)
        return carry

    loop(16, body, 0)


def buffers(size):
    shapes = {}

    def vmem(name, *shape):
        shapes[name] = pltpu.VMEM(shape, F32)

    for name in SWAP_FIELDS:
        planes, rows = FINE[int(name[1])]
        tall = padded_rows(rows)
        vmem(f"{name}_ext", planes + 2, tall, LANES)
        for part in ("yf", "yl", "yhi", "ylo"):
            vmem(f"{name}_{part}", planes, 1, LANES)
        for part in ("px", "xlo", "xhi", "side"):
            vmem(f"{name}_{part}", tall, LANES)
    vmem("f0", 6, 16, 32, LANES)
    vmem("d0", 16, 32, LANES)
    vmem("t0", 32, LANES)
    vmem("t1w", 64, LANES)
    vmem("k1", 8, 16, LANES)
    for level, (planes, rows, _) in RING.items():
        for kind in "wsvced":
            vmem(f"{kind}{level}", planes, rows, LANES)
        vmem(f"f{level}", 6, planes, rows, LANES)
        vmem(f"t{level}", rows, LANES)
    for name in ("w1", "s1"):
        vmem(f"{name}_px", 16, LANES)
        vmem(f"{name}_left", 3, 32, LANES)
        vmem(f"{name}_right", 3, 32, LANES)
    vmem("s4", 1, 4, LANES)
    vmem("k4", 1, 4, LANES)
    vmem("own3", 8, LANES)
    vmem("side3", 26, 8, LANES)
    for level, (planes, rows, _) in zip((4, 5, 6), COARSE):
        tall = padded_rows(rows)
        for kind in "wvc":
            vmem(f"{kind}{level}_ext", planes + 2, tall, LANES)
        vmem(f"f{level}", 6, planes, tall, LANES)
        vmem(f"d{level}", planes, tall, LANES)
        vmem(f"q{level}", planes, tall, LANES)
        vmem(f"e{level}", planes, tall, LANES)
        vmem(f"t{level}", tall, LANES)
        if level > 4:
            vmem(f"k{level}", planes, tall, LANES)
    vmem("g0", 1, LANES)
    vmem("g1", size["gy"], size["gx"], 1, LANES)
    vmem("g2", 8, LANES)
    vmem("g5", size["gz"], 8, LANES)
    vmem("g6", size["gx"] * size["gz"], 4 * LANES)
    shapes["send"] = pltpu.SemaphoreType.DMA((len(SWAP_FIELDS), 6))
    shapes["recv"] = pltpu.SemaphoreType.DMA((len(SWAP_FIELDS), 6))
    shapes["send_side"] = pltpu.SemaphoreType.DMA((2, 26))
    shapes["recv_side"] = pltpu.SemaphoreType.DMA((2, 26))
    for key, count in (("flat", size["gx"] * size["gy"]), ("side3", 26), ("gz", size["gz"])):
        shapes[f"send_{key}"] = pltpu.SemaphoreType.DMA((count,))
        shapes[f"recv_{key}"] = pltpu.SemaphoreType.DMA((count,))
    return shapes


def solution(mesh):
    size = dict(mesh.shape)
    spec = P("gz", "gx", "gy")

    def body(source, conductivity):
        shapes = buffers(size)
        block = jax.ShapeDtypeStruct(source.shape, F32)

        def run(*refs):
            kernel(size, tuple(shapes), *refs)

        return pl.pallas_call(
            run,
            out_shape=(block, block),
            in_specs=[pl.BlockSpec(memory_space=pltpu.VMEM)] * 2,
            out_specs=[pl.BlockSpec(memory_space=pltpu.VMEM)] * 2,
            scratch_shapes=list(shapes.values()),
            compiler_params=pltpu.CompilerParams(
                collective_id=0, has_side_effects=True, vmem_limit_bytes=48 * 1024 * 1024
            ),
        )(source, conductivity)

    return jax.shard_map(
        body, mesh=mesh, in_specs=(spec, spec), out_specs=(spec, spec), check_vma=False
    )
```

```python
import jax
import jax.numpy as jnp
from jax import lax
from jax.experimental import pallas as pl
from jax.experimental.pallas import tpu as pltpu
from jax.sharding import PartitionSpec as P

MESH = pl.DeviceIdType.MESH
AXES = ("gx", "gy", "gz")
OMEGA = 2.0 / 3.0
LANES = 128
F32 = jnp.float32

FINE = ((16, 32),)
RING = {1: (24, 32, 1), 2: (12, 16, 2), 3: (6, 8, 4)}
MARGIN = 8
COARSE = ((16, 16, 4), (8, 8, 8), (4, 4, 16))
SWAP_FIELDS = ("w0", "v0", "c0", "r0")
SIDES = tuple((a, b, c) for a in (-1, 0, 1) for b in (-1, 0, 1) for c in (-1, 0, 1) if (a, b, c) != (0, 0, 0))


def padded_rows(rows):
    return max(rows, 8)


def lane_of(shape):
    return lax.broadcasted_iota(jnp.int32, shape, len(shape) - 1)


def row_of(shape):
    return lax.broadcasted_iota(jnp.int32, shape, len(shape) - 2)


def loop(count, body, carry):
    if count <= 4:
        for i in range(count):
            carry = body(i, carry)
        return carry
    return lax.fori_loop(0, count, body, carry, unroll=2)


def shift_lanes(x, amount):
    amount = lax.rem(amount + LANES, LANES) if not isinstance(amount, int) else amount % LANES
    if isinstance(amount, int) and amount == 0:
        return x
    return pltpu.roll(x, amount, 1)


def one_hot(cond):
    return jnp.where(cond, 1.0, 0.0).astype(F32)


def exact_dot(a, b):
    return jnp.dot(a, b, precision=lax.Precision.HIGHEST, preferred_element_type=F32)


class Swap:
    def __init__(self, refs, sems, level, place):
        self.ext, self.yf, self.yl, self.yhi, self.ylo, self.px, self.xlo, self.xhi, self.side = refs
        self.send, self.recv = sems
        self.planes, self.rows = FINE[level]
        self.half = 2**level
        self.place = place
        self.copies = []

    def put(self, z, x, packed):
        self.ext[z + 1] = x
        self.yf[z] = x[0:1]
        self.yl[z] = x[self.rows - 1 : self.rows]
        moved = shift_lanes(x, 2 * self.half * z + self.half)
        return jnp.where(lane_of(x.shape) // (2 * self.half) == z, moved, packed)

    def empty(self):
        return jnp.zeros(self.px.shape, F32)

    def start(self, packed):
        self.px[...] = packed
        n = self.planes
        at, size = self.place
        moves = (
            ("gz", 1, self.ext.at[n], self.ext.at[0]),
            ("gz", -1, self.ext.at[1], self.ext.at[n + 1]),
            ("gx", 1, self.yl, self.ylo),
            ("gx", -1, self.yf, self.yhi),
            ("gy", 1, self.px, self.xlo),
            ("gy", -1, self.px, self.xhi),
        )
        for i, (axis, step, src, dst) in enumerate(moves):
            to = tuple(
                lax.rem(at[a] + step + size[a], size[a]) if a == axis else at[a] for a in AXES
            )
            copy = pltpu.make_async_remote_copy(
                src_ref=src,
                dst_ref=dst,
                send_sem=self.send.at[i],
                recv_sem=self.recv.at[i],
                device_id=to,
                device_id_type=MESH,
            )
            copy.start()
            self.copies.append(copy)

    def finish(self):
        at, size = self.place
        for copy in self.copies:
            copy.wait()
        n = self.planes
        self.ext[0] = jnp.where(at["gz"] > 0, self.ext[0], 0.0)
        self.ext[n + 1] = jnp.where(at["gz"] < size["gz"] - 1, self.ext[n + 1], 0.0)
        self.ylo[...] = jnp.where(at["gx"] > 0, self.ylo[...], 0.0)
        self.yhi[...] = jnp.where(at["gx"] < size["gx"] - 1, self.yhi[...], 0.0)
        low = jnp.where(at["gy"] > 0, self.xlo[...], 0.0)
        high = jnp.where(at["gy"] < size["gy"] - 1, self.xhi[...], 0.0)
        self.side[...] = jnp.where(lane_of(low.shape) % (2 * self.half) < self.half, low, high)

    def around(self, z):
        x = self.ext[z + 1]
        row, lane = row_of(x.shape), lane_of(x.shape)
        tall, half = x.shape[0], self.half
        side = shift_lanes(self.side[...], -(2 * half * z + half))
        return x, (
            self.ext[z],
            self.ext[z + 2],
            jnp.where(row == 0, self.ylo[z], pltpu.roll(x, 1, 0)),
            jnp.where(row == self.rows - 1, self.yhi[z], pltpu.roll(x, tall - 1, 0)),
            shift_lanes(jnp.where(lane >= LANES - half, side, x), half),
            shift_lanes(jnp.where(lane < half, side, x), -half),
        )


class Ring:
    def __init__(self, ext, level):
        self.ext = ext
        self.planes, self.rows, self.half = RING[level]

    def put(self, z, x, carry):
        self.ext[z] = x
        return carry

    def around(self, z):
        n = self.planes
        if isinstance(z, int):
            before, after = (z + n - 1) % n, (z + 1) % n
        else:
            before, after = lax.rem(z + n - 1, n), lax.rem(z + 1, n)
        x = self.ext[z]
        return x, (
            self.ext[before],
            self.ext[after],
            pltpu.roll(x, 1, 0),
            pltpu.roll(x, x.shape[0] - 1, 0),
            shift_lanes(x, self.half),
            shift_lanes(x, -self.half),
        )


def ring_loop(first, count, total, body):
    def step(i, carry):
        z = first + i
        body(z % total if isinstance(z, int) else lax.rem(z, total))
        return carry

    loop(count, step, 0)


class Margin:
    def __init__(self, ext, px, left, right, sems, place):
        self.ext, self.px, self.left, self.right = ext, px, left, right
        self.send, self.recv = sems
        self.place = place
        self.copies = []

    def start(self):
        lane = lane_of((16, LANES))
        packed = jnp.zeros((16, LANES), F32)
        for z in range(MARGIN):
            x = self.ext[z, 0:16]
            spot = lane // 16 == z
            packed = jnp.where(spot & (lane % 16 < 8), shift_lanes(x, 16 * z - 64), packed)
            packed = jnp.where(spot & (lane % 16 >= 8), shift_lanes(x, 16 * z), packed)
        self.px[...] = packed
        at, size = self.place
        rows_out = {-1: pl.ds(0, 8), 0: pl.ds(0, 16), 1: pl.ds(8, 8)}
        rows_in = {-1: pl.ds(16, 8), 0: pl.ds(0, 16), 1: pl.ds(24, 8)}
        planes_in = {-1: pl.ds(8, 8), 0: pl.ds(0, 8), 1: pl.ds(16, 8)}
        block_in = {-1: 1, 0: 0, 1: 2}
        order = sorted(range(26), key=lambda i: sum(map(abs, SIDES[i])))
        for i in order:
            dz, dx, dy = SIDES[i]
            if dy == 0:
                src = self.ext.at[pl.ds(0, 8), rows_out[dx], :]
                dst = self.ext.at[planes_in[dz], rows_in[dx], :]
            else:
                land = self.left if dy == 1 else self.right
                src = self.px.at[rows_out[dx], :]
                dst = land.at[block_in[dz], rows_in[dx], :]
            copy = pltpu.make_async_remote_copy(
                src_ref=src,
                dst_ref=dst,
                send_sem=self.send.at[i],
                recv_sem=self.recv.at[i],
                device_id=neighbour(self.place, dz, dx, dy),
                device_id_type=MESH,
            )
            copy.start()
            self.copies.append(copy)

    def finish(self):
        at, size = self.place
        for copy in self.copies:
            copy.wait()
        shape = (32, LANES)
        row, lane = row_of(shape), lane_of(shape)
        for block in range(3):
            z_ok = (True, at["gz"] < size["gz"] - 1, at["gz"] > 0)[block]
            ok = (row < 16) | ((row < 24) & (at["gx"] < size["gx"] - 1)) | ((row >= 24) & (at["gx"] > 0))
            if block > 0:
                ok = ok & z_ok
            low = ok & (lane < 8) & (at["gy"] > 0)
            high = ok & (lane >= 72) & (lane < 80) & (at["gy"] < size["gy"] - 1)
            own = ok & (lane >= 8) & (lane < 72)
            sides = jnp.where(lane % 16 < 8, self.left[block], self.right[block])
            self.left[block] = sides

            def body(i, carry, block=block, low=low, high=high, own=own):
                z = 8 * block + i
                sides = self.left[block]
                merged = jnp.where(own, self.ext[z], 0.0)
                merged = jnp.where(low, shift_lanes(sides, -16 * i), merged)
                merged = jnp.where(high, shift_lanes(sides, 64 - 16 * i), merged)
                self.ext[z] = merged
                return carry

            loop(8, body, 0)


def neighbour(place, dz, dx, dy):
    at, size = place
    step = {"gz": dz, "gx": dx, "gy": dy}
    return tuple(lax.rem(at[a] + step[a] + size[a], size[a]) if step[a] else at[a] for a in AXES)


class Whole:
    def __init__(self, ext, shape):
        self.ext = ext
        self.planes, self.rows, self.half = shape
        self.ext[0] = jnp.zeros(self.ext.shape[1:], F32)
        self.ext[self.planes + 1] = jnp.zeros(self.ext.shape[1:], F32)

    def put(self, z, x, packed):
        self.ext[z + 1] = x
        return packed

    def around(self, z):
        return beside(self.ext[z], self.ext[z + 1], self.ext[z + 2], self.rows, self.half)


def beside(before, x, after, rows, half):
    row, lane = row_of(x.shape), lane_of(x.shape)
    return x, (
        before,
        after,
        jnp.where(row == 0, 0.0, pltpu.roll(x, 1, 0)),
        jnp.where(row == rows - 1, 0.0, pltpu.roll(x, x.shape[0] - 1, 0)),
        shift_lanes(jnp.where(lane >= LANES - half, 0.0, x), half),
        shift_lanes(jnp.where(lane < half, 0.0, x), -half),
    )


def applied(around, faces, z):
    x, near = around
    total = faces[0, z] * (x - near[0])
    for q in range(1, 6):
        total = total + faces[q, z] * (x - near[q])
    return total


def face_weights(field, faces, rate, level):
    scale = 0.5 * 0.25**level

    def body(z, carry):
        x, near = field.around(z)
        diagonal = jnp.zeros_like(x)
        for q in range(6):
            weight = scale * (x + near[q])
            faces[q, z] = weight
            diagonal = diagonal + weight
        inside = x > 0.0
        rate[z] = jnp.where(inside, OMEGA / jnp.where(inside, diagonal, 1.0), 0.0)
        return carry

    loop(field.planes, body, 0)


def pair_down(total, rows, half, scratch):
    scratch[...] = total
    count = total.shape[0] // 2
    both = scratch[pl.ds(0, count, stride=2), :] + scratch[pl.ds(1, count, stride=2), :]
    lane = lane_of(both.shape)
    other = jnp.where(lane // half % 2 == 0, shift_lanes(both, -half), shift_lanes(both, half))
    return 0.125 * (both + other)


def spread(coarse, rows, scratch):
    count = scratch.shape[0] // 2
    scratch[pl.ds(0, count, stride=2), :] = coarse[0:count]
    scratch[pl.ds(1, count, stride=2), :] = coarse[0:count]
    return scratch[...]


def store_layer(dst, z, layer):
    dst[z, 0 : layer.shape[0]] = layer


def down(field, source, faces, level_half, target, scratch):
    def body(z, carry):
        total = None
        for part in range(2):
            i = 2 * z + part
            defect = source[i] - applied(field.around(i), faces, i)
            total = defect if total is None else total + defect
        store_layer(target, z, pair_down(total, field.rows, level_half, scratch))
        return carry

    loop(field.planes // 2, body, 0)


def first_relax(field, source, rate, packed):
    def body(z, carry):
        return field.put(z, rate[z] * source[z], carry)

    return loop(field.planes, body, packed)


def add_coarse(field, old, coarse_layer, packed, scratch):
    def body(z, carry):
        wide = spread(coarse_layer(z), field.rows, scratch)
        for part in range(2):
            i = 2 * z + part
            carry = field.put(i, old.ext[i + 1] + wide, carry)
        return carry

    return loop(field.planes // 2, body, packed)


def relax_into(field, source, faces, rate, put, carry):
    def body(z, carry):
        around = field.around(z)
        return put(z, around[0] + rate[z] * (source[z] - applied(around, faces, z)), carry)

    return loop(field.planes, body, carry)


def restrict_weights(layer, planes, rows, half, target, scratch):
    def body(z, carry):
        store_layer(target, z, pair_down(layer(2 * z) + layer(2 * z + 1), rows, half, scratch))
        return carry

    loop(planes // 2, body, 0)


def kernel(size, names, source_hbm, weight_hbm, out_ref, residual_ref, *scratch):
    ref = dict(zip(names, scratch))
    source_ref, weight_ref = ref["source"], ref["weight"]
    load_weight = pltpu.make_async_copy(weight_hbm, weight_ref, ref["load"].at[0])
    load_source = pltpu.make_async_copy(source_hbm, source_ref, ref["load"].at[1])
    at = {a: lax.axis_index(a) for a in AXES}
    place = (at, size)

    peers = set()
    peers.update((k, 0, 0) for k in range(1, size["gz"]))
    flat = [(i, j) for i in range(size["gx"]) for j in range(size["gy"]) if (i, j) != (0, 0)]
    peers.update((0, i, j) for i, j in flat)
    barrier = pltpu.get_barrier_semaphore()
    for step in sorted(peers):
        pl.semaphore_signal(
            barrier, inc=1, device_id=neighbour(place, *step), device_id_type=MESH
        )
    load_weight.start()
    load_source.start()

    swaps = {}
    for k, name in enumerate(SWAP_FIELDS):
        parts = ("ext", "yf", "yl", "yhi", "ylo", "px", "xlo", "xhi", "side")
        swaps[name] = Swap(
            tuple(ref[f"{name}_{part}"] for part in parts),
            (ref["send"].at[k], ref["recv"].at[k]),
            int(name[1]),
            place,
        )
    margins = {}
    for k, name in enumerate(("w1", "s1")):
        margins[name] = Margin(
            *(ref[f"{name}{part}"] for part in ("", "_px", "_left", "_right")),
            (ref["send_side"].at[k], ref["recv_side"].at[k]),
            place,
        )
    square = (LANES, LANES)
    to_ring = one_hot(row_of(square) == 2 * (lane_of(square) - MARGIN))

    def into_ring(two_lanes, ring):
        packed = exact_dot(two_lanes[...].reshape(LANES, LANES), to_ring)
        ring[0:8, 0:16] = packed.reshape(8, 16, LANES)

    tile = (8, LANES)
    lane, row = lane_of(tile), row_of(tile)

    def send(src, dst, key, i, step):
        copy = pltpu.make_async_remote_copy(
            src_ref=src,
            dst_ref=dst,
            send_sem=ref[f"send_{key}"].at[i],
            recv_sem=ref[f"recv_{key}"].at[i],
            device_id=neighbour(place, *step),
            device_id_type=MESH,
        )
        copy.start()
        return copy

    def gather_flat(kind, rows, first, width):
        own = jnp.concatenate([rows, jnp.zeros((6, LANES), F32)], 0)
        pick = one_hot(row_of(square) == first + lane_of(square) % 8 * width)
        shrunk = exact_dot(own, pick)
        line = jnp.sum(jnp.where(lane // 32 == row, shrunk, 0.0), axis=0, keepdims=True)
        src, dst = ref[f"g0{kind}"], ref[f"g1{kind}"]
        src[...] = line
        copies = [
            send(src, dst.at[at["gy"], at["gx"]], f"flat_{kind}", i, (0, dx, dy))
            for i, (dx, dy) in enumerate(flat)
        ]
        dst[at["gy"], at["gx"]] = line
        return copies

    def gather_gz(kind, copies):
        for copy in copies:
            copy.wait()
        lines, src, dst = ref[f"g1{kind}"], ref[f"g2{kind}"], ref[f"g5{kind}"]
        merged = jnp.zeros(tile, F32)
        for k in range(size["gy"]):
            rows = jnp.concatenate([lines[k, i] for i in range(size["gx"])], 0)
            merged = jnp.where(lane // 8 % 4 == k, rows, merged)
        src[...] = merged
        copies = [
            send(src, dst.at[at["gz"]], f"gz_{kind}", k, (k, 0, 0)) for k in range(1, size["gz"])
        ]
        dst[at["gz"]] = merged
        return copies

    def gather_end(kind, copies, target, first):
        for copy in copies:
            copy.wait()
        wide = (LANES, 2 * LANES)
        expand = one_hot(row_of(wide) == lane_of(wide) // LANES * 32 + lane_of(wide) % LANES // 4)
        ref["g6"][...] = exact_dot(ref[f"g5{kind}"][...].reshape(LANES, LANES), expand)

        def body(z, carry):
            block = ref["g6"][pl.ds(pl.multiple_of(8 * z, 8), 8), :]
            for part in range(2):
                rows = pl.ds(part, 8, stride=2)
                target[z + first, rows, :] = block[:, part * LANES : (part + 1) * LANES]
            return carry

        loop(16, body, 0)

    swap = swaps["w0"]
    load_weight.wait()
    packed = loop(16, lambda z, c: swap.put(z, weight_ref[z], c), swap.empty())
    pl.semaphore_wait(barrier, len(peers))
    swap.start(packed)
    restrict_weights(lambda z: weight_ref[z], 16, 32, 1, ref["k1"], ref["t0"])
    into_ring(ref["k1"], ref["w1"])
    restrict_weights(lambda z: ref["k1"][z], 8, 16, 2, ref["h2"], ref["u1"])
    restrict_weights(lambda z: ref["h2"][z], 4, 8, 4, ref["h3"], ref["u2"])
    restrict_weights(lambda z: ref["h3"][z], 2, 4, 8, ref["h4"], ref["u3"])
    load_source.wait()
    swap.finish()
    face_weights(swap, ref["f0"], ref["d0"], 0)
    swap = swaps["v0"]
    swap.start(first_relax(swap, source_ref, ref["d0"], swap.empty()))
    copies_w = gather_flat("w", ref["h4"][0], 0, 16)
    margins["w1"].start()
    rings = {}
    for level in (1, 2, 3):
        for kind in "wvc":
            rings[kind, level] = Ring(ref[f"{kind}{level}"], level)
    fields = {}
    for level in range(4, 7):
        for kind in "wvc":
            fields[kind, level] = Whole(ref[f"{kind}{level}_ext"], COARSE[level - 4])
    ref["k6"][...] = jnp.zeros(ref["k6"].shape, F32)
    ref["q6"][...] = jnp.zeros(ref["q6"].shape, F32)
    swap.finish()
    down(swap, source_ref, ref["f0"], 1, ref["k1"], ref["t0"])
    into_ring(ref["k1"], ref["s1"])
    margins["s1"].start()

    copies_w = gather_gz("w", copies_w)
    margins["w1"].finish()
    for level in (1, 2, 3):
        field = rings["w", level]
        face_weights(field, ref[f"f{level}"], ref[f"d{level}"], level)
        if level < 3:
            restrict_weights(
                lambda z, field=field: field.ext[z],
                field.planes,
                field.rows,
                field.half,
                ref[f"w{level + 1}"],
                ref[f"t{level}"],
            )
    margins["s1"].finish()

    spans = {1: ((0, 24), (9, 10)), 2: ((9, 10), (5, 4)), 3: ((5, 4), (0, 1))}
    for level in (1, 2, 3):
        field, faces, rate = rings["v", level], ref[f"f{level}"], ref[f"d{level}"]
        source = ref[f"s{level}"]
        (first, count), (low, pairs) = spans[level]

        def relax_plane(z, field=field, rate=rate, source=source):
            field.put(z, rate[z] * source[z], 0)

        ring_loop(first, count, field.planes, relax_plane)

        def pair(z, field=field, faces=faces, source=source, level=level):
            total = None
            for part in range(2):
                i = 2 * z + part
                defect = source[i] - applied(field.around(i), faces, i)
                total = defect if total is None else total + defect
            below = pair_down(total, field.rows, field.half, ref[f"t{level}"])
            store_layer(ref[f"s{level + 1}"], z, below)

        ring_loop(low, pairs, field.planes // 2, pair)

    copies_s = gather_flat("s", ref["s4"][0][0:2], MARGIN, 8)

    def stacked(name):
        return jnp.where(row < 4, ref[name][0], pltpu.roll(ref[name][1], 4, 0))

    ref["own3"][...] = jnp.where(
        lane < 64, shift_lanes(stacked("s3"), -MARGIN), shift_lanes(stacked("d3"), 64 - MARGIN)
    )
    side_copies = [
        send(ref["own3"], ref["side3"].at[i], "side3", i, SIDES[i]) for i in range(26)
    ]
    gather_end("w", copies_w, ref["w4_ext"], 1)
    for level in (4, 5):
        planes, rows, half = COARSE[level - 4]
        field = fields["w", level]
        target = ref[f"k{level + 1}"]
        restrict_weights(
            lambda z, field=field: field.ext[z + 1], planes, rows, half, target, ref[f"t{level}"]
        )
        for z in range(planes // 2):
            fields["w", level + 1].put(z, target[z], 0)
    for level in (4, 5, 6):
        face_weights(fields["w", level], ref[f"f{level}"], ref[f"d{level}"], level)
    copies_s = gather_gz("s", copies_s)

    for copy in side_copies:
        copy.wait()
    inside = {
        "gz": {0: True, 1: at["gz"] < size["gz"] - 1, -1: at["gz"] > 0},
        "gx": {0: True, 1: at["gx"] < size["gx"] - 1, -1: at["gx"] > 0},
        "gy": {0: True, 1: at["gy"] < size["gy"] - 1, -1: at["gy"] > 0},
    }

    def from_side(dz, dx, dy):
        if (dz, dx, dy) == (0, 0, 0):
            return ref["own3"][...]
        x = ref["side3"][SIDES.index((-dz, -dx, -dy))]
        for axis, step in (("gz", dz), ("gx", dx), ("gy", dy)):
            if step:
                x = jnp.where(inside[axis][step], x, 0.0)
        return x

    for block, dz in enumerate((0, 1, -1)):
        column = {}
        for dy in (-1, 0, 1):
            mid, up, low = (from_side(dz, dx, dy) for dx in (0, 1, -1))
            turn = lambda x: pltpu.roll(x, 4, 0)
            far = jnp.where(row < 6, turn(up), turn(low))
            column[0, dy] = jnp.where(row < 4, mid, far)
            far = jnp.where(row < 6, up, low)
            column[1, dy] = jnp.where(row < 4, turn(mid), far)
        for part in range(2):
            z = 2 * block + part
            mid = column[part, 0]
            for name, base in (("s3", 0), ("d3", 64)):
                ends = jnp.where(
                    lane < 8,
                    shift_lanes(column[part, -1], 72 - base),
                    shift_lanes(column[part, 1], 72 - base),
                )
                body = shift_lanes(mid, MARGIN - base)
                full = jnp.where((lane >= 8) & (lane < 72), body, jnp.where(lane < 80, ends, 0.0))
                ref[name][z] = full
            rings["v", 3].put(z, ref["d3"][z] * ref["s3"][z], 0)
    gather_end("s", copies_s, ref["q4"], 0)

    for level in (4, 5):
        field, faces = fields["v", level], ref[f"f{level}"]
        first_relax(field, ref[f"q{level}"], ref[f"d{level}"], 0)
        down(field, ref[f"q{level}"], faces, field.half, ref[f"q{level + 1}"], ref[f"t{level}"])

    planes, rows, half = COARSE[2]
    faces, rate, source = ref["f6"], ref["d6"], ref["q6"]
    zero = jnp.zeros((8, LANES), F32)

    def sweep(_, value):
        out = []
        for z in range(planes):
            before = value[z - 1] if z > 0 else zero
            after = value[z + 1] if z < planes - 1 else zero
            around = beside(before, value[z], after, rows, half)
            out.append(value[z] + rate[z] * (source[z] - applied(around, faces, z)))
        return tuple(out)

    start = tuple(rate[z] * source[z] for z in range(planes))
    bottom = lax.fori_loop(0, 7, sweep, start)
    for z in range(planes):
        ref["e6"][z] = bottom[z]
    for level in (5, 4):
        field = fields["c", level]
        coarse = ref[f"e{level + 1}"]
        add_coarse(
            field, fields["v", level], lambda z, c=coarse: c[z], 0, ref[f"t{level}"]
        )
        target = ref[f"e{level}"]

        def put(z, x, carry, target=target):
            target[z] = x
            return carry

        relax_into(field, ref[f"q{level}"], ref[f"f{level}"], ref[f"d{level}"], put, 0)

    pick_lane = one_hot(row_of(square) == (8 * at["gy"] - 1 + lane_of(square) // 8) * 4)
    coarse_row = (row_of((8, 16)) // 2 + 1) % 4 - 1
    pick_row = one_hot(lane_of((8, 16)) == 2 * at["gx"] + coarse_row)
    for block, dz in enumerate((0, 1, -1)):
        layer = ref["e4"][jnp.clip(at["gz"] + dz, 0, size["gz"] - 1)]
        if dz:
            layer = jnp.where(inside["gz"][dz], layer, 0.0)
        up = exact_dot(pick_row, exact_dot(layer, pick_lane))
        for part in range(2):
            z = 2 * block + part
            rings["c", 3].put(z, rings["v", 3].ext[z] + up, 0)

    for level, first, count in ((3, 5, 4), (2, 11, 6), (1, 23, 10)):
        field, faces, rate = rings["c", level], ref[f"f{level}"], ref[f"d{level}"]
        source, target = ref[f"s{level}"], ref[f"e{level}"]
        if level < 3:
            coarse, scratch = ref[f"e{level + 1}"], ref[f"t{level}"]

            def lift(z, field=field, coarse=coarse, scratch=scratch, level=level):
                wide = spread(coarse[z], field.rows, scratch)
                for part in range(2):
                    i = 2 * z + part
                    field.put(i, rings["v", level].ext[i] + wide, 0)

            ring_loop(first // 2, (count + 2) // 2, field.planes // 2, lift)

        def relax_plane(z, field=field, faces=faces, rate=rate, source=source, target=target):
            around = field.around(z)
            target[z] = around[0] + rate[z] * (source[z] - applied(around, faces, z))

        ring_loop(first, count, field.planes, relax_plane)

    to_fine = one_hot(row_of(square) == MARGIN + lane_of(square) // 2)
    swap, old = swaps["c0"], swaps["v0"]
    scratch = ref["t1w"]
    side = old.side[...]

    def lifted(zc):
        return spread(exact_dot(ref["e1"][zc], to_fine), 0, scratch)

    def lift(zc, side):
        layer = ref["e1"][zc]
        wide = spread(exact_dot(layer, to_fine), 0, scratch)
        at_lane = lane_of(square) // 4 == zc
        ends = one_hot(
            at_lane
            & (row_of(square) == jnp.where(lane_of(square) % 2 == 0, MARGIN - 1, MARGIN + 64))
        )
        side = side + spread(exact_dot(layer, ends), 0, scratch)[0:32]
        for part in range(2):
            i = 2 * zc + part
            swap.ext[i + 1] = old.ext[i + 1] + wide[0:32]
            swap.yhi[i] = old.yhi[i] + jnp.where(inside["gx"][1], wide[32:33], 0.0)
            swap.ylo[i] = old.ylo[i] + jnp.where(inside["gx"][-1], wide[63:64], 0.0)
        return side

    swap.side[...] = loop(8, lift, side)
    swap.ext[17] = old.ext[17] + lifted(8)[0:32]
    swap.ext[0] = old.ext[0] + lifted(23)[0:32]
    last = swaps["r0"]
    faces, rate = ref["f0"], ref["d0"]

    def put(z, x, carry):
        out_ref[z] = x
        return last.put(z, x, carry)

    last.start(relax_into(swap, source_ref, faces, rate, put, last.empty()))
    last.finish()

    def body(z, carry):
        residual_ref[z] = source_ref[z] - applied(last.around(z), faces, z)
        return carry

    loop(16, body, 0)


def buffers(size):
    shapes = {}

    def vmem(name, *shape):
        shapes[name] = pltpu.VMEM(shape, F32)

    for name in SWAP_FIELDS:
        planes, rows = FINE[int(name[1])]
        tall = padded_rows(rows)
        vmem(f"{name}_ext", planes + 2, tall, LANES)
        for part in ("yf", "yl", "yhi", "ylo"):
            vmem(f"{name}_{part}", planes, 1, LANES)
        for part in ("px", "xlo", "xhi", "side"):
            vmem(f"{name}_{part}", tall, LANES)
    vmem("f0", 6, 16, 32, LANES)
    vmem("d0", 16, 32, LANES)
    vmem("t0", 32, LANES)
    vmem("t1w", 64, LANES)
    vmem("k1", 8, 16, LANES)
    for level, (planes, rows, _) in RING.items():
        for kind in "wsvced":
            vmem(f"{kind}{level}", planes, rows, LANES)
        vmem(f"f{level}", 6, planes, rows, LANES)
        vmem(f"t{level}", rows, LANES)
    for name in ("w1", "s1"):
        vmem(f"{name}_px", 16, LANES)
        vmem(f"{name}_left", 3, 32, LANES)
        vmem(f"{name}_right", 3, 32, LANES)
    vmem("s4", 1, 4, LANES)
    vmem("source", 16, 32, LANES)
    vmem("weight", 16, 32, LANES)
    for level, rows in ((2, 8), (3, 4), (4, 2)):
        vmem(f"h{level}", 16 >> level, rows, LANES)
        vmem(f"u{level - 1}", 2 * rows, LANES)
    vmem("own3", 8, LANES)
    vmem("side3", 26, 8, LANES)
    for level, (planes, rows, _) in zip((4, 5, 6), COARSE):
        tall = padded_rows(rows)
        for kind in "wvc":
            vmem(f"{kind}{level}_ext", planes + 2, tall, LANES)
        vmem(f"f{level}", 6, planes, tall, LANES)
        vmem(f"d{level}", planes, tall, LANES)
        vmem(f"q{level}", planes, tall, LANES)
        vmem(f"e{level}", planes, tall, LANES)
        vmem(f"t{level}", tall, LANES)
        if level > 4:
            vmem(f"k{level}", planes, tall, LANES)
    for kind in "ws":
        vmem(f"g0{kind}", 1, LANES)
        vmem(f"g1{kind}", size["gy"], size["gx"], 1, LANES)
        vmem(f"g2{kind}", 8, LANES)
        vmem(f"g5{kind}", size["gz"], 8, LANES)
    vmem("g6", size["gx"] * size["gz"], 2 * LANES)
    shapes["load"] = pltpu.SemaphoreType.DMA((2,))
    shapes["send"] = pltpu.SemaphoreType.DMA((len(SWAP_FIELDS), 6))
    shapes["recv"] = pltpu.SemaphoreType.DMA((len(SWAP_FIELDS), 6))
    shapes["send_side"] = pltpu.SemaphoreType.DMA((2, 26))
    shapes["recv_side"] = pltpu.SemaphoreType.DMA((2, 26))
    counts = [("side3", 26)]
    for kind in "ws":
        counts += [(f"flat_{kind}", size["gx"] * size["gy"]), (f"gz_{kind}", size["gz"])]
    for key, count in counts:
        shapes[f"send_{key}"] = pltpu.SemaphoreType.DMA((count,))
        shapes[f"recv_{key}"] = pltpu.SemaphoreType.DMA((count,))
    return shapes


def solution(mesh):
    size = dict(mesh.shape)
    spec = P("gz", "gx", "gy")

    def body(source, conductivity):
        shapes = buffers(size)
        block = jax.ShapeDtypeStruct(source.shape, F32)

        def run(*refs):
            kernel(size, tuple(shapes), *refs)

        return pl.pallas_call(
            run,
            out_shape=(block, block),
            in_specs=[pl.BlockSpec(memory_space=pltpu.HBM)] * 2,
            out_specs=[pl.BlockSpec(memory_space=pltpu.VMEM)] * 2,
            scratch_shapes=list(shapes.values()),
            compiler_params=pltpu.CompilerParams(
                collective_id=0, has_side_effects=True, vmem_limit_bytes=48 * 1024 * 1024
            ),
        )(source, conductivity)

    return jax.shard_map(
        body, mesh=mesh, in_specs=(spec, spec), out_specs=(spec, spec), check_vma=False
    )
```

```python
import functools

import jax
import jax.numpy as jnp
from jax import lax
from jax.experimental import pallas as pl
from jax.experimental.pallas import tpu as pltpu
from jax.sharding import PartitionSpec as P

MESH = pl.DeviceIdType.MESH
AXES = ("gx", "gy", "gz")
OMEGA = 2.0 / 3.0
LANES = 128
F32 = jnp.float32

FINE = ((16, 32),)
RING = {1: (24, 32, 1), 2: (12, 16, 2), 3: (6, 8, 4)}
MARGIN = 8
COARSE = ((16, 16, 4), (8, 8, 8), (4, 4, 16))
SWAP_FIELDS = ("w0", "v0", "c0", "r0")
SIDES = tuple((a, b, c) for a in (-1, 0, 1) for b in (-1, 0, 1) for c in (-1, 0, 1) if (a, b, c) != (0, 0, 0))


def padded_rows(rows):
    return max(rows, 8)


def lane_of(shape):
    return lax.broadcasted_iota(jnp.int32, shape, len(shape) - 1)


def row_of(shape):
    return lax.broadcasted_iota(jnp.int32, shape, len(shape) - 2)


def loop(count, body, carry):
    if count <= 4:
        for i in range(count):
            carry = body(i, carry)
        return carry
    return lax.fori_loop(0, count, body, carry, unroll=2)


def shift_lanes(x, amount):
    amount = lax.rem(amount + LANES, LANES) if not isinstance(amount, int) else amount % LANES
    if isinstance(amount, int) and amount == 0:
        return x
    return pltpu.roll(x, amount, 1)


def one_hot(cond):
    return jnp.where(cond, 1.0, 0.0).astype(F32)


def exact_dot(a, b):
    return jnp.dot(a, b, precision=lax.Precision.HIGHEST, preferred_element_type=F32)


class Swap:
    def __init__(self, refs, sems, level, place):
        self.ext, self.yf, self.yl, self.yhi, self.ylo, self.px, self.xlo, self.xhi, self.side = refs
        self.send, self.recv = sems
        self.planes, self.rows = FINE[level]
        self.half = 2**level
        self.place = place
        self.copies = []

    def put(self, z, x, packed):
        self.ext[z + 1] = x
        self.yf[z] = x[0:1]
        self.yl[z] = x[self.rows - 1 : self.rows]
        moved = shift_lanes(x, 2 * self.half * z + self.half)
        return jnp.where(lane_of(x.shape) // (2 * self.half) == z, moved, packed)

    def empty(self):
        return jnp.zeros(self.px.shape, F32)

    def start(self, packed):
        self.px[...] = packed
        n = self.planes
        at, size = self.place
        moves = (
            ("gz", 1, self.ext.at[n], self.ext.at[0]),
            ("gz", -1, self.ext.at[1], self.ext.at[n + 1]),
            ("gx", 1, self.yl, self.ylo),
            ("gx", -1, self.yf, self.yhi),
            ("gy", 1, self.px, self.xlo),
            ("gy", -1, self.px, self.xhi),
        )
        for i, (axis, step, src, dst) in enumerate(moves):
            to = tuple(
                lax.rem(at[a] + step + size[a], size[a]) if a == axis else at[a] for a in AXES
            )
            copy = pltpu.make_async_remote_copy(
                src_ref=src,
                dst_ref=dst,
                send_sem=self.send.at[i],
                recv_sem=self.recv.at[i],
                device_id=to,
                device_id_type=MESH,
            )
            copy.start()
            self.copies.append(copy)

    def finish(self):
        at, size = self.place
        for copy in self.copies:
            copy.wait()
        n = self.planes
        self.ext[0] = jnp.where(at["gz"] > 0, self.ext[0], 0.0)
        self.ext[n + 1] = jnp.where(at["gz"] < size["gz"] - 1, self.ext[n + 1], 0.0)
        self.ylo[...] = jnp.where(at["gx"] > 0, self.ylo[...], 0.0)
        self.yhi[...] = jnp.where(at["gx"] < size["gx"] - 1, self.yhi[...], 0.0)
        low = jnp.where(at["gy"] > 0, self.xlo[...], 0.0)
        high = jnp.where(at["gy"] < size["gy"] - 1, self.xhi[...], 0.0)
        self.side[...] = jnp.where(lane_of(low.shape) % (2 * self.half) < self.half, low, high)

    def around(self, z):
        x = self.ext[z + 1]
        row, lane = row_of(x.shape), lane_of(x.shape)
        tall, half = x.shape[0], self.half
        side = shift_lanes(self.side[...], -(2 * half * z + half))
        return x, (
            self.ext[z],
            self.ext[z + 2],
            jnp.where(row == 0, self.ylo[z], pltpu.roll(x, 1, 0)),
            jnp.where(row == self.rows - 1, self.yhi[z], pltpu.roll(x, tall - 1, 0)),
            shift_lanes(jnp.where(lane >= LANES - half, side, x), half),
            shift_lanes(jnp.where(lane < half, side, x), -half),
        )


class Ring:
    def __init__(self, ext, level):
        self.ext = ext
        self.planes, self.rows, self.half = RING[level]

    def put(self, z, x, carry):
        self.ext[z] = x
        return carry

    def around(self, z):
        n = self.planes
        if isinstance(z, int):
            before, after = (z + n - 1) % n, (z + 1) % n
        else:
            before, after = lax.rem(z + n - 1, n), lax.rem(z + 1, n)
        x = self.ext[z]
        return x, (
            self.ext[before],
            self.ext[after],
            pltpu.roll(x, 1, 0),
            pltpu.roll(x, x.shape[0] - 1, 0),
            shift_lanes(x, self.half),
            shift_lanes(x, -self.half),
        )


def ring_loop(first, count, total, body):
    def step(i, carry):
        z = first + i
        body(z % total if isinstance(z, int) else lax.rem(z, total))
        return carry

    loop(count, step, 0)


class Margin:
    def __init__(self, ext, px, left, right, pairs, land, sems, place):
        self.ext, self.px, self.left, self.right = ext, px, left, right
        self.pairs, self.land = pairs, land
        self.send, self.recv = sems
        self.place = place
        self.copies = []

    def start(self):
        lane = lane_of((16, LANES))
        packed = jnp.zeros((16, LANES), F32)
        for z in range(MARGIN):
            x = self.ext[z, 0:16]
            spot = lane // 16 == z
            packed = jnp.where(spot & (lane % 16 < 8), shift_lanes(x, 16 * z - 64), packed)
            packed = jnp.where(spot & (lane % 16 >= 8), shift_lanes(x, 16 * z), packed)
        self.px[...] = packed
        for z in range(4):
            first = shift_lanes(self.ext[z, 0:16], -MARGIN)
            second = shift_lanes(self.ext[z + 4, 0:16], 64 - MARGIN)
            self.pairs[z] = jnp.where(lane < 64, first, second)
        rows_out = {-1: pl.ds(0, 8), 0: pl.ds(0, 16), 1: pl.ds(8, 8)}
        rows_in = {-1: pl.ds(16, 8), 0: pl.ds(0, 16), 1: pl.ds(24, 8)}
        block_in = {-1: 1, 0: 0, 1: 2}
        order = sorted(range(26), key=lambda i: sum(map(abs, SIDES[i])))
        for i in order:
            dz, dx, dy = SIDES[i]
            if dy == 0:
                src = self.pairs.at[:, rows_out[dx], :]
                dst = self.land.at[block_in[dz], :, rows_in[dx], :]
            else:
                land = self.left if dy == 1 else self.right
                src = self.px.at[rows_out[dx], :]
                dst = land.at[block_in[dz], rows_in[dx], :]
            copy = pltpu.make_async_remote_copy(
                src_ref=src,
                dst_ref=dst,
                send_sem=self.send.at[i],
                recv_sem=self.recv.at[i],
                device_id=neighbour(self.place, dz, dx, dy),
                device_id_type=MESH,
            )
            copy.start()
            self.copies.append(copy)

    def finish(self):
        at, size = self.place
        for copy in self.copies:
            copy.wait()
        shape = (32, LANES)
        row, lane = row_of(shape), lane_of(shape)
        for block in range(3):
            z_ok = (True, at["gz"] < size["gz"] - 1, at["gz"] > 0)[block]
            ok = (row < 16) | ((row < 24) & (at["gx"] < size["gx"] - 1)) | ((row >= 24) & (at["gx"] > 0))
            if block > 0:
                ok = ok & z_ok
            low = ok & (lane < 8) & (at["gy"] > 0)
            high = ok & (lane >= 72) & (lane < 80) & (at["gy"] < size["gy"] - 1)
            own = ok & (lane >= 8) & (lane < 72)
            sides = jnp.where(lane % 16 < 8, self.left[block], self.right[block])
            self.left[block] = sides

            def body(j, carry, block=block, low=low, high=high, own=own, half=0):
                i = j + 4 * half
                z = 8 * block + i
                sides = self.left[block]
                middle = shift_lanes(self.land[block, j], MARGIN - 64 * half)
                if block == 0:
                    middle = jnp.where(row < 16, self.ext[z], middle)
                merged = jnp.where(own, middle, 0.0)
                merged = jnp.where(low, shift_lanes(sides, -16 * i), merged)
                merged = jnp.where(high, shift_lanes(sides, 64 - 16 * i), merged)
                self.ext[z] = merged
                return carry

            for half in range(2):
                loop(4, functools.partial(body, half=half), 0)


def neighbour(place, dz, dx, dy):
    at, size = place
    step = {"gz": dz, "gx": dx, "gy": dy}
    return tuple(lax.rem(at[a] + step[a] + size[a], size[a]) if step[a] else at[a] for a in AXES)


class Whole:
    def __init__(self, ext, shape):
        self.ext = ext
        self.planes, self.rows, self.half = shape
        self.ext[0] = jnp.zeros(self.ext.shape[1:], F32)
        self.ext[self.planes + 1] = jnp.zeros(self.ext.shape[1:], F32)

    def put(self, z, x, packed):
        self.ext[z + 1] = x
        return packed

    def around(self, z):
        return beside(self.ext[z], self.ext[z + 1], self.ext[z + 2], self.rows, self.half)


def beside(before, x, after, rows, half):
    row, lane = row_of(x.shape), lane_of(x.shape)
    return x, (
        before,
        after,
        jnp.where(row == 0, 0.0, pltpu.roll(x, 1, 0)),
        jnp.where(row == rows - 1, 0.0, pltpu.roll(x, x.shape[0] - 1, 0)),
        shift_lanes(jnp.where(lane >= LANES - half, 0.0, x), half),
        shift_lanes(jnp.where(lane < half, 0.0, x), -half),
    )


def applied(around, faces, z):
    x, near = around
    total = faces[0, z] * (x - near[0])
    for q in range(1, 6):
        total = total + faces[q, z] * (x - near[q])
    return total


def face_weights(field, faces, rate, level):
    scale = 0.5 * 0.25**level

    def body(z, carry):
        x, near = field.around(z)
        diagonal = jnp.zeros_like(x)
        for q in range(6):
            weight = scale * (x + near[q])
            faces[q, z] = weight
            diagonal = diagonal + weight
        inside = x > 0.0
        rate[z] = jnp.where(inside, OMEGA / jnp.where(inside, diagonal, 1.0), 0.0)
        return carry

    loop(field.planes, body, 0)


def pair_down(total, rows, half, scratch):
    scratch[...] = total
    count = total.shape[0] // 2
    both = scratch[pl.ds(0, count, stride=2), :] + scratch[pl.ds(1, count, stride=2), :]
    lane = lane_of(both.shape)
    other = jnp.where(lane // half % 2 == 0, shift_lanes(both, -half), shift_lanes(both, half))
    return 0.125 * (both + other)


def spread(coarse, rows, scratch):
    count = scratch.shape[0] // 2
    scratch[pl.ds(0, count, stride=2), :] = coarse[0:count]
    scratch[pl.ds(1, count, stride=2), :] = coarse[0:count]
    return scratch[...]


def store_layer(dst, z, layer):
    dst[z, 0 : layer.shape[0]] = layer


def down(field, source, faces, level_half, target, scratch):
    def body(z, carry):
        total = None
        for part in range(2):
            i = 2 * z + part
            defect = source[i] - applied(field.around(i), faces, i)
            total = defect if total is None else total + defect
        store_layer(target, z, pair_down(total, field.rows, level_half, scratch))
        return carry

    loop(field.planes // 2, body, 0)


def first_relax(field, source, rate, packed):
    def body(z, carry):
        return field.put(z, rate[z] * source[z], carry)

    return loop(field.planes, body, packed)


def add_coarse(field, old, coarse_layer, packed, scratch):
    def body(z, carry):
        wide = spread(coarse_layer(z), field.rows, scratch)
        for part in range(2):
            i = 2 * z + part
            carry = field.put(i, old.ext[i + 1] + wide, carry)
        return carry

    return loop(field.planes // 2, body, packed)


def relax_into(field, source, faces, rate, put, carry):
    def body(z, carry):
        around = field.around(z)
        return put(z, around[0] + rate[z] * (source[z] - applied(around, faces, z)), carry)

    return loop(field.planes, body, carry)


def restrict_weights(layer, planes, rows, half, target, scratch):
    def body(z, carry):
        store_layer(target, z, pair_down(layer(2 * z) + layer(2 * z + 1), rows, half, scratch))
        return carry

    loop(planes // 2, body, 0)


def kernel(size, names, source_hbm, weight_hbm, out_hbm, residual_hbm, *scratch):
    ref = dict(zip(names, scratch))
    source_ref, weight_ref = ref["source"], ref["weight"]
    load_weight = pltpu.make_async_copy(weight_hbm, weight_ref, ref["load"].at[0])
    load_source = pltpu.make_async_copy(source_hbm, source_ref, ref["load"].at[1])
    out_ref, residual_ref = ref["out"], ref["residual"]
    at = {a: lax.axis_index(a) for a in AXES}
    place = (at, size)

    peers = set()
    peers.update((k, 0, 0) for k in range(1, size["gz"]))
    flat = [(i, j) for i in range(size["gx"]) for j in range(size["gy"]) if (i, j) != (0, 0)]
    peers.update((0, i, j) for i, j in flat)
    barrier = pltpu.get_barrier_semaphore()
    for step in sorted(peers):
        pl.semaphore_signal(
            barrier, inc=1, device_id=neighbour(place, *step), device_id_type=MESH
        )
    load_weight.start()
    load_source.start()

    swaps = {}
    for k, name in enumerate(SWAP_FIELDS):
        parts = ("ext", "yf", "yl", "yhi", "ylo", "px", "xlo", "xhi", "side")
        swaps[name] = Swap(
            tuple(ref[f"{name}_{part}"] for part in parts),
            (ref["send"].at[k], ref["recv"].at[k]),
            int(name[1]),
            place,
        )
    margins = {}
    for k, name in enumerate(("w1", "s1")):
        margins[name] = Margin(
            *(ref[f"{name}{part}"] for part in ("", "_px", "_left", "_right", "_pairs", "_land")),
            (ref["send_side"].at[k], ref["recv_side"].at[k]),
            place,
        )
    square = (LANES, LANES)
    to_ring = one_hot(row_of(square) == 2 * (lane_of(square) - MARGIN))

    def into_ring(two_lanes, ring):
        packed = exact_dot(two_lanes[...].reshape(LANES, LANES), to_ring)
        ring[0:8, 0:16] = packed.reshape(8, 16, LANES)

    tile = (8, LANES)
    lane, row = lane_of(tile), row_of(tile)

    def send(src, dst, key, i, step):
        copy = pltpu.make_async_remote_copy(
            src_ref=src,
            dst_ref=dst,
            send_sem=ref[f"send_{key}"].at[i],
            recv_sem=ref[f"recv_{key}"].at[i],
            device_id=neighbour(place, *step),
            device_id_type=MESH,
        )
        copy.start()
        return copy

    def gather_flat(kind, rows, first, width):
        own = jnp.concatenate([rows, jnp.zeros((6, LANES), F32)], 0)
        pick = one_hot(row_of(square) == first + lane_of(square) % 8 * width)
        shrunk = exact_dot(own, pick)
        line = jnp.sum(jnp.where(lane // 32 == row, shrunk, 0.0), axis=0, keepdims=True)
        src, dst = ref[f"g0{kind}"], ref[f"g1{kind}"]
        src[...] = line
        copies = [
            send(src, dst.at[at["gy"], at["gx"]], f"flat_{kind}", i, (0, dx, dy))
            for i, (dx, dy) in enumerate(flat)
        ]
        dst[at["gy"], at["gx"]] = line
        return copies

    def gather_gz(kind, copies):
        for copy in copies:
            copy.wait()
        lines, src, dst = ref[f"g1{kind}"], ref[f"g2{kind}"], ref[f"g5{kind}"]
        merged = jnp.zeros(tile, F32)
        for k in range(size["gy"]):
            rows = jnp.concatenate([lines[k, i] for i in range(size["gx"])], 0)
            merged = jnp.where(lane // 8 % 4 == k, rows, merged)
        src[...] = merged
        copies = [
            send(src, dst.at[at["gz"]], f"gz_{kind}", k, (k, 0, 0)) for k in range(1, size["gz"])
        ]
        dst[at["gz"]] = merged
        return copies

    def gather_end(kind, copies, target, first):
        for copy in copies:
            copy.wait()
        wide = (LANES, 2 * LANES)
        expand = one_hot(row_of(wide) == lane_of(wide) // LANES * 32 + lane_of(wide) % LANES // 4)
        ref["g6"][...] = exact_dot(ref[f"g5{kind}"][...].reshape(LANES, LANES), expand)

        def body(z, carry):
            block = ref["g6"][pl.ds(pl.multiple_of(8 * z, 8), 8), :]
            for part in range(2):
                rows = pl.ds(part, 8, stride=2)
                target[z + first, rows, :] = block[:, part * LANES : (part + 1) * LANES]
            return carry

        loop(16, body, 0)

    swap = swaps["w0"]
    load_weight.wait()
    packed = loop(16, lambda z, c: swap.put(z, weight_ref[z], c), swap.empty())
    pl.semaphore_wait(barrier, len(peers))
    swap.start(packed)
    restrict_weights(lambda z: weight_ref[z], 16, 32, 1, ref["k1"], ref["t0"])
    into_ring(ref["k1"], ref["w1"])
    restrict_weights(lambda z: ref["k1"][z], 8, 16, 2, ref["h2"], ref["u1"])
    restrict_weights(lambda z: ref["h2"][z], 4, 8, 4, ref["h3"], ref["u2"])
    restrict_weights(lambda z: ref["h3"][z], 2, 4, 8, ref["h4"], ref["u3"])
    load_source.wait()
    swap.finish()
    face_weights(swap, ref["f0"], ref["d0"], 0)
    swap = swaps["v0"]
    swap.start(first_relax(swap, source_ref, ref["d0"], swap.empty()))
    copies_w = gather_flat("w", ref["h4"][0], 0, 16)
    margins["w1"].start()
    rings = {}
    for level in (1, 2, 3):
        for kind in "wvc":
            rings[kind, level] = Ring(ref[f"{kind}{level}"], level)
    fields = {}
    for level in range(4, 7):
        for kind in "wvc":
            fields[kind, level] = Whole(ref[f"{kind}{level}_ext"], COARSE[level - 4])
    ref["k6"][...] = jnp.zeros(ref["k6"].shape, F32)
    ref["q6"][...] = jnp.zeros(ref["q6"].shape, F32)
    swap.finish()
    down(swap, source_ref, ref["f0"], 1, ref["k1"], ref["t0"])
    into_ring(ref["k1"], ref["s1"])
    margins["s1"].start()

    copies_w = gather_gz("w", copies_w)
    margins["w1"].finish()
    for level in (1, 2, 3):
        field = rings["w", level]
        face_weights(field, ref[f"f{level}"], ref[f"d{level}"], level)
        if level < 3:
            restrict_weights(
                lambda z, field=field: field.ext[z],
                field.planes,
                field.rows,
                field.half,
                ref[f"w{level + 1}"],
                ref[f"t{level}"],
            )
    margins["s1"].finish()

    spans = {1: ((0, 24), (9, 10)), 2: ((9, 10), (5, 4)), 3: ((5, 4), (0, 1))}
    for level in (1, 2, 3):
        field, faces, rate = rings["v", level], ref[f"f{level}"], ref[f"d{level}"]
        source = ref[f"s{level}"]
        (first, count), (low, pairs) = spans[level]

        def relax_plane(z, field=field, rate=rate, source=source):
            field.put(z, rate[z] * source[z], 0)

        ring_loop(first, count, field.planes, relax_plane)

        def pair(z, field=field, faces=faces, source=source, level=level):
            total = None
            for part in range(2):
                i = 2 * z + part
                defect = source[i] - applied(field.around(i), faces, i)
                total = defect if total is None else total + defect
            below = pair_down(total, field.rows, field.half, ref[f"t{level}"])
            store_layer(ref[f"s{level + 1}"], z, below)

        ring_loop(low, pairs, field.planes // 2, pair)

    copies_s = gather_flat("s", ref["s4"][0][0:2], MARGIN, 8)

    def stacked(name):
        return jnp.where(row < 4, ref[name][0], pltpu.roll(ref[name][1], 4, 0))

    ref["own3"][...] = jnp.where(
        lane < 64, shift_lanes(stacked("s3"), -MARGIN), shift_lanes(stacked("d3"), 64 - MARGIN)
    )
    side_copies = [
        send(ref["own3"], ref["side3"].at[i], "side3", i, SIDES[i]) for i in range(26)
    ]
    gather_end("w", copies_w, ref["w4_ext"], 1)
    for level in (4, 5):
        planes, rows, half = COARSE[level - 4]
        field = fields["w", level]
        target = ref[f"k{level + 1}"]
        restrict_weights(
            lambda z, field=field: field.ext[z + 1], planes, rows, half, target, ref[f"t{level}"]
        )
        for z in range(planes // 2):
            fields["w", level + 1].put(z, target[z], 0)
    for level in (4, 5, 6):
        face_weights(fields["w", level], ref[f"f{level}"], ref[f"d{level}"], level)
    copies_s = gather_gz("s", copies_s)

    for copy in side_copies:
        copy.wait()
    inside = {
        "gz": {0: True, 1: at["gz"] < size["gz"] - 1, -1: at["gz"] > 0},
        "gx": {0: True, 1: at["gx"] < size["gx"] - 1, -1: at["gx"] > 0},
        "gy": {0: True, 1: at["gy"] < size["gy"] - 1, -1: at["gy"] > 0},
    }

    def from_side(dz, dx, dy):
        if (dz, dx, dy) == (0, 0, 0):
            return ref["own3"][...]
        x = ref["side3"][SIDES.index((-dz, -dx, -dy))]
        for axis, step in (("gz", dz), ("gx", dx), ("gy", dy)):
            if step:
                x = jnp.where(inside[axis][step], x, 0.0)
        return x

    for block, dz in enumerate((0, 1, -1)):
        column = {}
        for dy in (-1, 0, 1):
            mid, up, low = (from_side(dz, dx, dy) for dx in (0, 1, -1))
            turn = lambda x: pltpu.roll(x, 4, 0)
            far = jnp.where(row < 6, turn(up), turn(low))
            column[0, dy] = jnp.where(row < 4, mid, far)
            far = jnp.where(row < 6, up, low)
            column[1, dy] = jnp.where(row < 4, turn(mid), far)
        for part in range(2):
            z = 2 * block + part
            mid = column[part, 0]
            for name, base in (("s3", 0), ("d3", 64)):
                ends = jnp.where(
                    lane < 8,
                    shift_lanes(column[part, -1], 72 - base),
                    shift_lanes(column[part, 1], 72 - base),
                )
                body = shift_lanes(mid, MARGIN - base)
                full = jnp.where((lane >= 8) & (lane < 72), body, jnp.where(lane < 80, ends, 0.0))
                ref[name][z] = full
            rings["v", 3].put(z, ref["d3"][z] * ref["s3"][z], 0)
    gather_end("s", copies_s, ref["q4"], 0)

    for level in (4, 5):
        field, faces = fields["v", level], ref[f"f{level}"]
        first_relax(field, ref[f"q{level}"], ref[f"d{level}"], 0)
        down(field, ref[f"q{level}"], faces, field.half, ref[f"q{level + 1}"], ref[f"t{level}"])

    planes, rows, half = COARSE[2]
    faces, rate, source = ref["f6"], ref["d6"], ref["q6"]
    zero = jnp.zeros((8, LANES), F32)

    def sweep(_, value):
        out = []
        for z in range(planes):
            before = value[z - 1] if z > 0 else zero
            after = value[z + 1] if z < planes - 1 else zero
            around = beside(before, value[z], after, rows, half)
            out.append(value[z] + rate[z] * (source[z] - applied(around, faces, z)))
        return tuple(out)

    start = tuple(rate[z] * source[z] for z in range(planes))
    bottom = lax.fori_loop(0, 7, sweep, start)
    for z in range(planes):
        ref["e6"][z] = bottom[z]
    for level in (5, 4):
        field = fields["c", level]
        coarse = ref[f"e{level + 1}"]
        add_coarse(
            field, fields["v", level], lambda z, c=coarse: c[z], 0, ref[f"t{level}"]
        )
        target = ref[f"e{level}"]

        def put(z, x, carry, target=target):
            target[z] = x
            return carry

        relax_into(field, ref[f"q{level}"], ref[f"f{level}"], ref[f"d{level}"], put, 0)

    pick_lane = one_hot(row_of(square) == (8 * at["gy"] - 1 + lane_of(square) // 8) * 4)
    coarse_row = (row_of((8, 16)) // 2 + 1) % 4 - 1
    pick_row = one_hot(lane_of((8, 16)) == 2 * at["gx"] + coarse_row)
    for block, dz in enumerate((0, 1, -1)):
        layer = ref["e4"][jnp.clip(at["gz"] + dz, 0, size["gz"] - 1)]
        if dz:
            layer = jnp.where(inside["gz"][dz], layer, 0.0)
        up = exact_dot(pick_row, exact_dot(layer, pick_lane))
        for part in range(2):
            z = 2 * block + part
            rings["c", 3].put(z, rings["v", 3].ext[z] + up, 0)

    for level, first, count in ((3, 5, 4), (2, 11, 6), (1, 23, 10)):
        field, faces, rate = rings["c", level], ref[f"f{level}"], ref[f"d{level}"]
        source, target = ref[f"s{level}"], ref[f"e{level}"]
        if level < 3:
            coarse, scratch = ref[f"e{level + 1}"], ref[f"t{level}"]

            def lift(z, field=field, coarse=coarse, scratch=scratch, level=level):
                wide = spread(coarse[z], field.rows, scratch)
                for part in range(2):
                    i = 2 * z + part
                    field.put(i, rings["v", level].ext[i] + wide, 0)

            ring_loop(first // 2, (count + 2) // 2, field.planes // 2, lift)

        def relax_plane(z, field=field, faces=faces, rate=rate, source=source, target=target):
            around = field.around(z)
            target[z] = around[0] + rate[z] * (source[z] - applied(around, faces, z))

        ring_loop(first, count, field.planes, relax_plane)

    to_fine = one_hot(row_of(square) == MARGIN + lane_of(square) // 2)
    swap, old = swaps["c0"], swaps["v0"]
    scratch = ref["t1w"]
    side = old.side[...]

    def lifted(zc):
        return spread(exact_dot(ref["e1"][zc], to_fine), 0, scratch)

    def lift(zc, side):
        layer = ref["e1"][zc]
        wide = spread(exact_dot(layer, to_fine), 0, scratch)
        at_lane = lane_of(square) // 4 == zc
        ends = one_hot(
            at_lane
            & (row_of(square) == jnp.where(lane_of(square) % 2 == 0, MARGIN - 1, MARGIN + 64))
        )
        side = side + spread(exact_dot(layer, ends), 0, scratch)[0:32]
        for part in range(2):
            i = 2 * zc + part
            swap.ext[i + 1] = old.ext[i + 1] + wide[0:32]
            swap.yhi[i] = old.yhi[i] + jnp.where(inside["gx"][1], wide[32:33], 0.0)
            swap.ylo[i] = old.ylo[i] + jnp.where(inside["gx"][-1], wide[63:64], 0.0)
        return side

    swap.side[...] = loop(8, lift, side)
    swap.ext[17] = old.ext[17] + lifted(8)[0:32]
    swap.ext[0] = old.ext[0] + lifted(23)[0:32]
    last = swaps["r0"]
    faces, rate = ref["f0"], ref["d0"]

    def put(z, x, carry):
        out_ref[z] = x
        return last.put(z, x, carry)

    last.start(relax_into(swap, source_ref, faces, rate, put, last.empty()))
    stores = [pltpu.make_async_copy(out_ref, out_hbm, ref["load"].at[2])]
    stores[0].start()
    last.finish()

    def body(z, carry):
        residual_ref[z] = source_ref[z] - applied(last.around(z), faces, z)
        return carry

    for half in range(2):
        lax.fori_loop(8 * half, 8 * half + 8, body, 0, unroll=2)
        part = pl.ds(8 * half, 8)
        store = pltpu.make_async_copy(
            residual_ref.at[part], residual_hbm.at[part], ref["load"].at[3 + half]
        )
        store.start()
        stores.append(store)
    for store in stores:
        store.wait()


def buffers(size):
    shapes = {}

    def vmem(name, *shape):
        shapes[name] = pltpu.VMEM(shape, F32)

    for name in SWAP_FIELDS:
        planes, rows = FINE[int(name[1])]
        tall = padded_rows(rows)
        vmem(f"{name}_ext", planes + 2, tall, LANES)
        for part in ("yf", "yl", "yhi", "ylo"):
            vmem(f"{name}_{part}", planes, 1, LANES)
        for part in ("px", "xlo", "xhi", "side"):
            vmem(f"{name}_{part}", tall, LANES)
    vmem("f0", 6, 16, 32, LANES)
    vmem("d0", 16, 32, LANES)
    vmem("t0", 32, LANES)
    vmem("t1w", 64, LANES)
    vmem("k1", 8, 16, LANES)
    for level, (planes, rows, _) in RING.items():
        for kind in "wsvced":
            vmem(f"{kind}{level}", planes, rows, LANES)
        vmem(f"f{level}", 6, planes, rows, LANES)
        vmem(f"t{level}", rows, LANES)
    for name in ("w1", "s1"):
        vmem(f"{name}_px", 16, LANES)
        vmem(f"{name}_pairs", 4, 16, LANES)
        vmem(f"{name}_land", 3, 4, 32, LANES)
        vmem(f"{name}_left", 3, 32, LANES)
        vmem(f"{name}_right", 3, 32, LANES)
    vmem("s4", 1, 4, LANES)
    vmem("source", 16, 32, LANES)
    vmem("weight", 16, 32, LANES)
    vmem("out", 16, 32, LANES)
    vmem("residual", 16, 32, LANES)
    for level, rows in ((2, 8), (3, 4), (4, 2)):
        vmem(f"h{level}", 16 >> level, rows, LANES)
        vmem(f"u{level - 1}", 2 * rows, LANES)
    vmem("own3", 8, LANES)
    vmem("side3", 26, 8, LANES)
    for level, (planes, rows, _) in zip((4, 5, 6), COARSE):
        tall = padded_rows(rows)
        for kind in "wvc":
            vmem(f"{kind}{level}_ext", planes + 2, tall, LANES)
        vmem(f"f{level}", 6, planes, tall, LANES)
        vmem(f"d{level}", planes, tall, LANES)
        vmem(f"q{level}", planes, tall, LANES)
        vmem(f"e{level}", planes, tall, LANES)
        vmem(f"t{level}", tall, LANES)
        if level > 4:
            vmem(f"k{level}", planes, tall, LANES)
    for kind in "ws":
        vmem(f"g0{kind}", 1, LANES)
        vmem(f"g1{kind}", size["gy"], size["gx"], 1, LANES)
        vmem(f"g2{kind}", 8, LANES)
        vmem(f"g5{kind}", size["gz"], 8, LANES)
    vmem("g6", size["gx"] * size["gz"], 2 * LANES)
    shapes["load"] = pltpu.SemaphoreType.DMA((5,))
    shapes["send"] = pltpu.SemaphoreType.DMA((len(SWAP_FIELDS), 6))
    shapes["recv"] = pltpu.SemaphoreType.DMA((len(SWAP_FIELDS), 6))
    shapes["send_side"] = pltpu.SemaphoreType.DMA((2, 26))
    shapes["recv_side"] = pltpu.SemaphoreType.DMA((2, 26))
    counts = [("side3", 26)]
    for kind in "ws":
        counts += [(f"flat_{kind}", size["gx"] * size["gy"]), (f"gz_{kind}", size["gz"])]
    for key, count in counts:
        shapes[f"send_{key}"] = pltpu.SemaphoreType.DMA((count,))
        shapes[f"recv_{key}"] = pltpu.SemaphoreType.DMA((count,))
    return shapes


def solution(mesh):
    size = dict(mesh.shape)
    spec = P("gz", "gx", "gy")

    def body(source, conductivity):
        shapes = buffers(size)
        block = jax.ShapeDtypeStruct(source.shape, F32)

        def run(*refs):
            kernel(size, tuple(shapes), *refs)

        return pl.pallas_call(
            run,
            out_shape=(block, block),
            in_specs=[pl.BlockSpec(memory_space=pltpu.HBM)] * 2,
            out_specs=[pl.BlockSpec(memory_space=pltpu.HBM)] * 2,
            scratch_shapes=list(shapes.values()),
            compiler_params=pltpu.CompilerParams(
                collective_id=0, has_side_effects=True, vmem_limit_bytes=63 * 1024 * 1024
            ),
        )(source, conductivity)

    return jax.shard_map(
        body, mesh=mesh, in_specs=(spec, spec), out_specs=(spec, spec), check_vma=False
    )
```

```python
import functools

import jax
import jax.numpy as jnp
from jax import lax
from jax.experimental import pallas as pl
from jax.experimental.pallas import tpu as pltpu
from jax.sharding import PartitionSpec as P

MESH = pl.DeviceIdType.MESH
AXES = ("gx", "gy", "gz")
OMEGA = 2.0 / 3.0
LANES = 128
F32 = jnp.float32

FINE = ((16, 32),)
RING = {1: (24, 32, 1), 2: (12, 16, 2), 3: (6, 8, 4)}
MARGIN = 8
COARSE = ((16, 16, 4), (8, 8, 8), (4, 4, 16))
SWAP_FIELDS = ("w0", "v0", "c0", "r0")
SIDES = tuple((a, b, c) for a in (-1, 0, 1) for b in (-1, 0, 1) for c in (-1, 0, 1) if (a, b, c) != (0, 0, 0))


def padded_rows(rows):
    return max(rows, 8)


def lane_of(shape):
    return lax.broadcasted_iota(jnp.int32, shape, len(shape) - 1)


def row_of(shape):
    return lax.broadcasted_iota(jnp.int32, shape, len(shape) - 2)


def loop(count, body, carry):
    if count <= 4:
        for i in range(count):
            carry = body(i, carry)
        return carry
    return lax.fori_loop(0, count, body, carry, unroll=True)


def shift_lanes(x, amount):
    amount = lax.rem(amount + LANES, LANES) if not isinstance(amount, int) else amount % LANES
    if isinstance(amount, int) and amount == 0:
        return x
    return pltpu.roll(x, amount, 1)


def one_hot(cond):
    return jnp.where(cond, 1.0, 0.0).astype(F32)


def exact_dot(a, b):
    return jnp.dot(a, b, precision=lax.Precision.HIGHEST, preferred_element_type=F32)


class Swap:
    def __init__(self, refs, sems, level, place):
        self.ext, self.yf, self.yl, self.yhi, self.ylo, self.px, self.xlo, self.xhi, self.side = refs
        self.send, self.recv = sems
        self.planes, self.rows = FINE[level]
        self.half = 2**level
        self.place = place
        self.copies = []

    def put(self, z, x, packed):
        self.ext[z + 1] = x
        self.yf[z] = x[0:1]
        self.yl[z] = x[self.rows - 1 : self.rows]
        moved = shift_lanes(x, 2 * self.half * z + self.half)
        return jnp.where(lane_of(x.shape) // (2 * self.half) == z, moved, packed)

    def empty(self):
        return jnp.zeros(self.px.shape, F32)

    def start(self, packed):
        self.px[...] = packed
        n = self.planes
        at, size = self.place
        moves = (
            ("gz", 1, self.ext.at[n], self.ext.at[0]),
            ("gz", -1, self.ext.at[1], self.ext.at[n + 1]),
            ("gx", 1, self.yl, self.ylo),
            ("gx", -1, self.yf, self.yhi),
            ("gy", 1, self.px, self.xlo),
            ("gy", -1, self.px, self.xhi),
        )
        for i, (axis, step, src, dst) in enumerate(moves):
            to = tuple(
                lax.rem(at[a] + step + size[a], size[a]) if a == axis else at[a] for a in AXES
            )
            copy = pltpu.make_async_remote_copy(
                src_ref=src,
                dst_ref=dst,
                send_sem=self.send.at[i],
                recv_sem=self.recv.at[i],
                device_id=to,
                device_id_type=MESH,
            )
            copy.start()
            self.copies.append(copy)

    def finish(self):
        at, size = self.place
        for copy in self.copies:
            copy.wait()
        n = self.planes
        self.ext[0] = jnp.where(at["gz"] > 0, self.ext[0], 0.0)
        self.ext[n + 1] = jnp.where(at["gz"] < size["gz"] - 1, self.ext[n + 1], 0.0)
        self.ylo[...] = jnp.where(at["gx"] > 0, self.ylo[...], 0.0)
        self.yhi[...] = jnp.where(at["gx"] < size["gx"] - 1, self.yhi[...], 0.0)
        low = jnp.where(at["gy"] > 0, self.xlo[...], 0.0)
        high = jnp.where(at["gy"] < size["gy"] - 1, self.xhi[...], 0.0)
        self.side[...] = jnp.where(lane_of(low.shape) % (2 * self.half) < self.half, low, high)

    def around(self, z):
        x = self.ext[z + 1]
        row, lane = row_of(x.shape), lane_of(x.shape)
        tall, half = x.shape[0], self.half
        side = shift_lanes(self.side[...], -(2 * half * z + half))
        return x, (
            self.ext[z],
            self.ext[z + 2],
            jnp.where(row == 0, self.ylo[z], pltpu.roll(x, 1, 0)),
            jnp.where(row == self.rows - 1, self.yhi[z], pltpu.roll(x, tall - 1, 0)),
            shift_lanes(jnp.where(lane >= LANES - half, side, x), half),
            shift_lanes(jnp.where(lane < half, side, x), -half),
        )


class Ring:
    def __init__(self, ext, level):
        self.ext = ext
        self.planes, self.rows, self.half = RING[level]

    def put(self, z, x, carry):
        self.ext[z] = x
        return carry

    def around(self, z):
        n = self.planes
        if isinstance(z, int):
            before, after = (z + n - 1) % n, (z + 1) % n
        else:
            before, after = lax.rem(z + n - 1, n), lax.rem(z + 1, n)
        x = self.ext[z]
        return x, (
            self.ext[before],
            self.ext[after],
            pltpu.roll(x, 1, 0),
            pltpu.roll(x, x.shape[0] - 1, 0),
            shift_lanes(x, self.half),
            shift_lanes(x, -self.half),
        )


def ring_loop(first, count, total, body):
    def step(i, carry):
        z = first + i
        body(z % total if isinstance(z, int) else lax.rem(z, total))
        return carry

    loop(count, step, 0)


class Margin:
    def __init__(self, ext, px, left, right, pairs, land, sems, place):
        self.ext, self.px, self.left, self.right = ext, px, left, right
        self.pairs, self.land = pairs, land
        self.send, self.recv = sems
        self.place = place
        self.copies = []

    def start(self):
        lane = lane_of((16, LANES))
        packed = jnp.zeros((16, LANES), F32)
        for z in range(MARGIN):
            x = self.ext[z, 0:16]
            spot = lane // 16 == z
            packed = jnp.where(spot & (lane % 16 < 8), shift_lanes(x, 16 * z - 64), packed)
            packed = jnp.where(spot & (lane % 16 >= 8), shift_lanes(x, 16 * z), packed)
        self.px[...] = packed
        for z in range(4):
            first = shift_lanes(self.ext[z, 0:16], -MARGIN)
            second = shift_lanes(self.ext[z + 4, 0:16], 64 - MARGIN)
            self.pairs[z] = jnp.where(lane < 64, first, second)
        rows_out = {-1: pl.ds(0, 8), 0: pl.ds(0, 16), 1: pl.ds(8, 8)}
        rows_in = {-1: pl.ds(16, 8), 0: pl.ds(0, 16), 1: pl.ds(24, 8)}
        block_in = {-1: 1, 0: 0, 1: 2}
        order = sorted(range(26), key=lambda i: sum(map(abs, SIDES[i])))
        for i in order:
            dz, dx, dy = SIDES[i]
            if dy == 0:
                src = self.pairs.at[:, rows_out[dx], :]
                dst = self.land.at[block_in[dz], :, rows_in[dx], :]
            else:
                land = self.left if dy == 1 else self.right
                src = self.px.at[rows_out[dx], :]
                dst = land.at[block_in[dz], rows_in[dx], :]
            copy = pltpu.make_async_remote_copy(
                src_ref=src,
                dst_ref=dst,
                send_sem=self.send.at[i],
                recv_sem=self.recv.at[i],
                device_id=neighbour(self.place, dz, dx, dy),
                device_id_type=MESH,
            )
            copy.start()
            self.copies.append(copy)

    def finish(self):
        at, size = self.place
        for copy in self.copies:
            copy.wait()
        shape = (32, LANES)
        row, lane = row_of(shape), lane_of(shape)
        for block in range(3):
            z_ok = (True, at["gz"] < size["gz"] - 1, at["gz"] > 0)[block]
            ok = (row < 16) | ((row < 24) & (at["gx"] < size["gx"] - 1)) | ((row >= 24) & (at["gx"] > 0))
            if block > 0:
                ok = ok & z_ok
            low = ok & (lane < 8) & (at["gy"] > 0)
            high = ok & (lane >= 72) & (lane < 80) & (at["gy"] < size["gy"] - 1)
            own = ok & (lane >= 8) & (lane < 72)
            sides = jnp.where(lane % 16 < 8, self.left[block], self.right[block])
            self.left[block] = sides

            def body(j, carry, block=block, low=low, high=high, own=own, half=0):
                i = j + 4 * half
                z = 8 * block + i
                sides = self.left[block]
                middle = shift_lanes(self.land[block, j], MARGIN - 64 * half)
                if block == 0:
                    middle = jnp.where(row < 16, self.ext[z], middle)
                merged = jnp.where(own, middle, 0.0)
                merged = jnp.where(low, shift_lanes(sides, -16 * i), merged)
                merged = jnp.where(high, shift_lanes(sides, 64 - 16 * i), merged)
                self.ext[z] = merged
                return carry

            for half in range(2):
                loop(4, functools.partial(body, half=half), 0)


def neighbour(place, dz, dx, dy):
    at, size = place
    step = {"gz": dz, "gx": dx, "gy": dy}
    return tuple(lax.rem(at[a] + step[a] + size[a], size[a]) if step[a] else at[a] for a in AXES)


class Whole:
    def __init__(self, ext, shape):
        self.ext = ext
        self.planes, self.rows, self.half = shape
        self.ext[0] = jnp.zeros(self.ext.shape[1:], F32)
        self.ext[self.planes + 1] = jnp.zeros(self.ext.shape[1:], F32)

    def put(self, z, x, packed):
        self.ext[z + 1] = x
        return packed

    def around(self, z):
        return beside(self.ext[z], self.ext[z + 1], self.ext[z + 2], self.rows, self.half)


def beside(before, x, after, rows, half):
    row, lane = row_of(x.shape), lane_of(x.shape)
    return x, (
        before,
        after,
        jnp.where(row == 0, 0.0, pltpu.roll(x, 1, 0)),
        jnp.where(row == rows - 1, 0.0, pltpu.roll(x, x.shape[0] - 1, 0)),
        shift_lanes(jnp.where(lane >= LANES - half, 0.0, x), half),
        shift_lanes(jnp.where(lane < half, 0.0, x), -half),
    )


def applied(around, faces, z):
    x, near = around
    total = faces[0, z] * (x - near[0])
    for q in range(1, 6):
        total = total + faces[q, z] * (x - near[q])
    return total


def face_weights(field, faces, rate, level):
    scale = 0.5 * 0.25**level

    def body(z, carry):
        x, near = field.around(z)
        diagonal = jnp.zeros_like(x)
        for q in range(6):
            weight = scale * (x + near[q])
            faces[q, z] = weight
            diagonal = diagonal + weight
        inside = x > 0.0
        rate[z] = jnp.where(inside, OMEGA / jnp.where(inside, diagonal, 1.0), 0.0)
        return carry

    loop(field.planes, body, 0)


def pair_down(total, rows, half, scratch):
    scratch[...] = total
    count = total.shape[0] // 2
    both = scratch[pl.ds(0, count, stride=2), :] + scratch[pl.ds(1, count, stride=2), :]
    lane = lane_of(both.shape)
    other = jnp.where(lane // half % 2 == 0, shift_lanes(both, -half), shift_lanes(both, half))
    return 0.125 * (both + other)


def spread(coarse, rows, scratch):
    count = scratch.shape[0] // 2
    scratch[pl.ds(0, count, stride=2), :] = coarse[0:count]
    scratch[pl.ds(1, count, stride=2), :] = coarse[0:count]
    return scratch[...]


def store_layer(dst, z, layer):
    dst[z, 0 : layer.shape[0]] = layer


def down(field, source, faces, level_half, target, scratch):
    def body(z, carry):
        total = None
        for part in range(2):
            i = 2 * z + part
            defect = source[i] - applied(field.around(i), faces, i)
            total = defect if total is None else total + defect
        store_layer(target, z, pair_down(total, field.rows, level_half, scratch))
        return carry

    loop(field.planes // 2, body, 0)


def first_relax(field, source, rate, packed):
    def body(z, carry):
        return field.put(z, rate[z] * source[z], carry)

    return loop(field.planes, body, packed)


def add_coarse(field, old, coarse_layer, packed, scratch):
    def body(z, carry):
        wide = spread(coarse_layer(z), field.rows, scratch)
        for part in range(2):
            i = 2 * z + part
            carry = field.put(i, old.ext[i + 1] + wide, carry)
        return carry

    return loop(field.planes // 2, body, packed)


def relax_into(field, source, faces, rate, put, carry):
    def body(z, carry):
        around = field.around(z)
        return put(z, around[0] + rate[z] * (source[z] - applied(around, faces, z)), carry)

    return loop(field.planes, body, carry)


def restrict_weights(layer, planes, rows, half, target, scratch):
    def body(z, carry):
        store_layer(target, z, pair_down(layer(2 * z) + layer(2 * z + 1), rows, half, scratch))
        return carry

    loop(planes // 2, body, 0)


def kernel(size, names, source_hbm, weight_hbm, out_hbm, residual_hbm, *scratch):
    ref = dict(zip(names, scratch))
    source_ref, weight_ref = ref["source"], ref["weight"]
    load_weight = pltpu.make_async_copy(weight_hbm, weight_ref, ref["load"].at[0])
    load_source = pltpu.make_async_copy(source_hbm, source_ref, ref["load"].at[1])
    out_ref, residual_ref = ref["out"], ref["residual"]
    at = {a: lax.axis_index(a) for a in AXES}
    place = (at, size)

    peers = set()
    peers.update((k, 0, 0) for k in range(1, size["gz"]))
    flat = [(i, j) for i in range(size["gx"]) for j in range(size["gy"]) if (i, j) != (0, 0)]
    peers.update((0, i, j) for i, j in flat)
    barrier = pltpu.get_barrier_semaphore()
    for step in sorted(peers):
        pl.semaphore_signal(
            barrier, inc=1, device_id=neighbour(place, *step), device_id_type=MESH
        )
    load_weight.start()
    load_source.start()

    swaps = {}
    for k, name in enumerate(SWAP_FIELDS):
        parts = ("ext", "yf", "yl", "yhi", "ylo", "px", "xlo", "xhi", "side")
        swaps[name] = Swap(
            tuple(ref[f"{name}_{part}"] for part in parts),
            (ref["send"].at[k], ref["recv"].at[k]),
            int(name[1]),
            place,
        )
    margins = {}
    for k, name in enumerate(("w1", "s1")):
        margins[name] = Margin(
            *(ref[f"{name}{part}"] for part in ("", "_px", "_left", "_right", "_pairs", "_land")),
            (ref["send_side"].at[k], ref["recv_side"].at[k]),
            place,
        )
    square = (LANES, LANES)
    to_ring = one_hot(row_of(square) == 2 * (lane_of(square) - MARGIN))

    def into_ring(two_lanes, ring):
        packed = exact_dot(two_lanes[...].reshape(LANES, LANES), to_ring)
        ring[0:8, 0:16] = packed.reshape(8, 16, LANES)

    tile = (8, LANES)
    lane, row = lane_of(tile), row_of(tile)

    def send(src, dst, key, i, step):
        copy = pltpu.make_async_remote_copy(
            src_ref=src,
            dst_ref=dst,
            send_sem=ref[f"send_{key}"].at[i],
            recv_sem=ref[f"recv_{key}"].at[i],
            device_id=neighbour(place, *step),
            device_id_type=MESH,
        )
        copy.start()
        return copy

    def gather_flat(kind, rows, first, width):
        own = jnp.concatenate([rows, jnp.zeros((6, LANES), F32)], 0)
        pick = one_hot(row_of(square) == first + lane_of(square) % 8 * width)
        shrunk = exact_dot(own, pick)
        line = jnp.sum(jnp.where(lane // 32 == row, shrunk, 0.0), axis=0, keepdims=True)
        src, dst = ref[f"g0{kind}"], ref[f"g1{kind}"]
        src[...] = line
        copies = [
            send(src, dst.at[at["gy"], at["gx"]], f"flat_{kind}", i, (0, dx, dy))
            for i, (dx, dy) in enumerate(flat)
        ]
        dst[at["gy"], at["gx"]] = line
        return copies

    def gather_gz(kind, copies):
        for copy in copies:
            copy.wait()
        lines, src, dst = ref[f"g1{kind}"], ref[f"g2{kind}"], ref[f"g5{kind}"]
        merged = jnp.zeros(tile, F32)
        for k in range(size["gy"]):
            rows = jnp.concatenate([lines[k, i] for i in range(size["gx"])], 0)
            merged = jnp.where(lane // 8 % 4 == k, rows, merged)
        src[...] = merged
        copies = [
            send(src, dst.at[at["gz"]], f"gz_{kind}", k, (k, 0, 0)) for k in range(1, size["gz"])
        ]
        dst[at["gz"]] = merged
        return copies

    def gather_end(kind, copies, target, first):
        for copy in copies:
            copy.wait()
        wide = (LANES, 2 * LANES)
        expand = one_hot(row_of(wide) == lane_of(wide) // LANES * 32 + lane_of(wide) % LANES // 4)
        ref["g6"][...] = exact_dot(ref[f"g5{kind}"][...].reshape(LANES, LANES), expand)

        def body(z, carry):
            block = ref["g6"][pl.ds(pl.multiple_of(8 * z, 8), 8), :]
            for part in range(2):
                rows = pl.ds(part, 8, stride=2)
                target[z + first, rows, :] = block[:, part * LANES : (part + 1) * LANES]
            return carry

        loop(16, body, 0)

    swap = swaps["w0"]
    load_weight.wait()
    packed = loop(16, lambda z, c: swap.put(z, weight_ref[z], c), swap.empty())
    pl.semaphore_wait(barrier, len(peers))
    swap.start(packed)
    restrict_weights(lambda z: weight_ref[z], 16, 32, 1, ref["k1"], ref["t0"])
    into_ring(ref["k1"], ref["w1"])
    restrict_weights(lambda z: ref["k1"][z], 8, 16, 2, ref["h2"], ref["u1"])
    restrict_weights(lambda z: ref["h2"][z], 4, 8, 4, ref["h3"], ref["u2"])
    restrict_weights(lambda z: ref["h3"][z], 2, 4, 8, ref["h4"], ref["u3"])
    load_source.wait()
    swap.finish()
    face_weights(swap, ref["f0"], ref["d0"], 0)
    swap = swaps["v0"]
    swap.start(first_relax(swap, source_ref, ref["d0"], swap.empty()))
    copies_w = gather_flat("w", ref["h4"][0], 0, 16)
    margins["w1"].start()
    rings = {}
    for level in (1, 2, 3):
        for kind in "wvc":
            rings[kind, level] = Ring(ref[f"{kind}{level}"], level)
    fields = {}
    for level in range(4, 7):
        for kind in "wvc":
            fields[kind, level] = Whole(ref[f"{kind}{level}_ext"], COARSE[level - 4])
    ref["k6"][...] = jnp.zeros(ref["k6"].shape, F32)
    ref["q6"][...] = jnp.zeros(ref["q6"].shape, F32)
    swap.finish()
    down(swap, source_ref, ref["f0"], 1, ref["k1"], ref["t0"])
    into_ring(ref["k1"], ref["s1"])
    margins["s1"].start()

    copies_w = gather_gz("w", copies_w)
    margins["w1"].finish()
    for level in (1, 2, 3):
        field = rings["w", level]
        face_weights(field, ref[f"f{level}"], ref[f"d{level}"], level)
        if level < 3:
            restrict_weights(
                lambda z, field=field: field.ext[z],
                field.planes,
                field.rows,
                field.half,
                ref[f"w{level + 1}"],
                ref[f"t{level}"],
            )
    margins["s1"].finish()

    spans = {1: ((0, 24), (9, 10)), 2: ((9, 10), (5, 4)), 3: ((5, 4), (0, 1))}
    for level in (1, 2, 3):
        field, faces, rate = rings["v", level], ref[f"f{level}"], ref[f"d{level}"]
        source = ref[f"s{level}"]
        (first, count), (low, pairs) = spans[level]

        def relax_plane(z, field=field, rate=rate, source=source):
            field.put(z, rate[z] * source[z], 0)

        ring_loop(first, count, field.planes, relax_plane)

        def pair(z, field=field, faces=faces, source=source, level=level):
            total = None
            for part in range(2):
                i = 2 * z + part
                defect = source[i] - applied(field.around(i), faces, i)
                total = defect if total is None else total + defect
            below = pair_down(total, field.rows, field.half, ref[f"t{level}"])
            store_layer(ref[f"s{level + 1}"], z, below)

        ring_loop(low, pairs, field.planes // 2, pair)

    copies_s = gather_flat("s", ref["s4"][0][0:2], MARGIN, 8)

    def stacked(name):
        return jnp.where(row < 4, ref[name][0], pltpu.roll(ref[name][1], 4, 0))

    ref["own3"][...] = jnp.where(
        lane < 64, shift_lanes(stacked("s3"), -MARGIN), shift_lanes(stacked("d3"), 64 - MARGIN)
    )
    side_copies = [
        send(ref["own3"], ref["side3"].at[i], "side3", i, SIDES[i]) for i in range(26)
    ]
    gather_end("w", copies_w, ref["w4_ext"], 1)
    for level in (4, 5):
        planes, rows, half = COARSE[level - 4]
        field = fields["w", level]
        target = ref[f"k{level + 1}"]
        restrict_weights(
            lambda z, field=field: field.ext[z + 1], planes, rows, half, target, ref[f"t{level}"]
        )
        for z in range(planes // 2):
            fields["w", level + 1].put(z, target[z], 0)
    for level in (4, 5, 6):
        face_weights(fields["w", level], ref[f"f{level}"], ref[f"d{level}"], level)
    copies_s = gather_gz("s", copies_s)

    for copy in side_copies:
        copy.wait()
    inside = {
        "gz": {0: True, 1: at["gz"] < size["gz"] - 1, -1: at["gz"] > 0},
        "gx": {0: True, 1: at["gx"] < size["gx"] - 1, -1: at["gx"] > 0},
        "gy": {0: True, 1: at["gy"] < size["gy"] - 1, -1: at["gy"] > 0},
    }

    def from_side(dz, dx, dy):
        if (dz, dx, dy) == (0, 0, 0):
            return ref["own3"][...]
        x = ref["side3"][SIDES.index((-dz, -dx, -dy))]
        for axis, step in (("gz", dz), ("gx", dx), ("gy", dy)):
            if step:
                x = jnp.where(inside[axis][step], x, 0.0)
        return x

    for block, dz in enumerate((0, 1, -1)):
        column = {}
        for dy in (-1, 0, 1):
            mid, up, low = (from_side(dz, dx, dy) for dx in (0, 1, -1))
            turn = lambda x: pltpu.roll(x, 4, 0)
            far = jnp.where(row < 6, turn(up), turn(low))
            column[0, dy] = jnp.where(row < 4, mid, far)
            far = jnp.where(row < 6, up, low)
            column[1, dy] = jnp.where(row < 4, turn(mid), far)
        for part in range(2):
            z = 2 * block + part
            mid = column[part, 0]
            for name, base in (("s3", 0), ("d3", 64)):
                ends = jnp.where(
                    lane < 8,
                    shift_lanes(column[part, -1], 72 - base),
                    shift_lanes(column[part, 1], 72 - base),
                )
                body = shift_lanes(mid, MARGIN - base)
                full = jnp.where((lane >= 8) & (lane < 72), body, jnp.where(lane < 80, ends, 0.0))
                ref[name][z] = full
            rings["v", 3].put(z, ref["d3"][z] * ref["s3"][z], 0)
    gather_end("s", copies_s, ref["q4"], 0)

    for level in (4, 5):
        field, faces = fields["v", level], ref[f"f{level}"]
        first_relax(field, ref[f"q{level}"], ref[f"d{level}"], 0)
        down(field, ref[f"q{level}"], faces, field.half, ref[f"q{level + 1}"], ref[f"t{level}"])

    planes, rows, half = COARSE[2]
    faces, rate, source = ref["f6"], ref["d6"], ref["q6"]
    zero = jnp.zeros((8, LANES), F32)

    def sweep(_, value):
        out = []
        for z in range(planes):
            before = value[z - 1] if z > 0 else zero
            after = value[z + 1] if z < planes - 1 else zero
            around = beside(before, value[z], after, rows, half)
            out.append(value[z] + rate[z] * (source[z] - applied(around, faces, z)))
        return tuple(out)

    start = tuple(rate[z] * source[z] for z in range(planes))
    bottom = lax.fori_loop(0, 7, sweep, start)
    for z in range(planes):
        ref["e6"][z] = bottom[z]
    for level in (5, 4):
        field = fields["c", level]
        coarse = ref[f"e{level + 1}"]
        add_coarse(
            field, fields["v", level], lambda z, c=coarse: c[z], 0, ref[f"t{level}"]
        )
        target = ref[f"e{level}"]

        def put(z, x, carry, target=target):
            target[z] = x
            return carry

        relax_into(field, ref[f"q{level}"], ref[f"f{level}"], ref[f"d{level}"], put, 0)

    pick_lane = one_hot(row_of(square) == (8 * at["gy"] - 1 + lane_of(square) // 8) * 4)
    coarse_row = (row_of((8, 16)) // 2 + 1) % 4 - 1
    pick_row = one_hot(lane_of((8, 16)) == 2 * at["gx"] + coarse_row)
    for block, dz in enumerate((0, 1, -1)):
        layer = ref["e4"][jnp.clip(at["gz"] + dz, 0, size["gz"] - 1)]
        if dz:
            layer = jnp.where(inside["gz"][dz], layer, 0.0)
        up = exact_dot(pick_row, exact_dot(layer, pick_lane))
        for part in range(2):
            z = 2 * block + part
            rings["c", 3].put(z, rings["v", 3].ext[z] + up, 0)

    for level, first, count in ((3, 5, 4), (2, 11, 6), (1, 23, 10)):
        field, faces, rate = rings["c", level], ref[f"f{level}"], ref[f"d{level}"]
        source, target = ref[f"s{level}"], ref[f"e{level}"]
        if level < 3:
            coarse, scratch = ref[f"e{level + 1}"], ref[f"t{level}"]

            def lift(z, field=field, coarse=coarse, scratch=scratch, level=level):
                wide = spread(coarse[z], field.rows, scratch)
                for part in range(2):
                    i = 2 * z + part
                    field.put(i, rings["v", level].ext[i] + wide, 0)

            ring_loop(first // 2, (count + 2) // 2, field.planes // 2, lift)

        def relax_plane(z, field=field, faces=faces, rate=rate, source=source, target=target):
            around = field.around(z)
            target[z] = around[0] + rate[z] * (source[z] - applied(around, faces, z))

        ring_loop(first, count, field.planes, relax_plane)

    to_fine = one_hot(row_of(square) == MARGIN + lane_of(square) // 2)
    swap, old = swaps["c0"], swaps["v0"]
    scratch = ref["t1w"]
    side = old.side[...]

    def lifted(zc):
        return spread(exact_dot(ref["e1"][zc], to_fine), 0, scratch)

    def lift(zc, side):
        layer = ref["e1"][zc]
        wide = spread(exact_dot(layer, to_fine), 0, scratch)
        at_lane = lane_of(square) // 4 == zc
        ends = one_hot(
            at_lane
            & (row_of(square) == jnp.where(lane_of(square) % 2 == 0, MARGIN - 1, MARGIN + 64))
        )
        side = side + spread(exact_dot(layer, ends), 0, scratch)[0:32]
        for part in range(2):
            i = 2 * zc + part
            swap.ext[i + 1] = old.ext[i + 1] + wide[0:32]
            swap.yhi[i] = old.yhi[i] + jnp.where(inside["gx"][1], wide[32:33], 0.0)
            swap.ylo[i] = old.ylo[i] + jnp.where(inside["gx"][-1], wide[63:64], 0.0)
        return side

    swap.side[...] = loop(8, lift, side)
    swap.ext[17] = old.ext[17] + lifted(8)[0:32]
    swap.ext[0] = old.ext[0] + lifted(23)[0:32]
    last = swaps["r0"]
    faces, rate = ref["f0"], ref["d0"]

    def put(z, x, carry):
        out_ref[z] = x
        return last.put(z, x, carry)

    last.start(relax_into(swap, source_ref, faces, rate, put, last.empty()))
    stores = [pltpu.make_async_copy(out_ref, out_hbm, ref["load"].at[2])]
    stores[0].start()
    last.finish()

    def body(z, carry):
        residual_ref[z] = source_ref[z] - applied(last.around(z), faces, z)
        return carry

    for half in range(2):
        lax.fori_loop(8 * half, 8 * half + 8, body, 0, unroll=8)
        part = pl.ds(8 * half, 8)
        store = pltpu.make_async_copy(
            residual_ref.at[part], residual_hbm.at[part], ref["load"].at[3 + half]
        )
        store.start()
        stores.append(store)
    for store in stores:
        store.wait()


def buffers(size):
    shapes = {}

    def vmem(name, *shape):
        shapes[name] = pltpu.VMEM(shape, F32)

    for name in SWAP_FIELDS:
        planes, rows = FINE[int(name[1])]
        tall = padded_rows(rows)
        vmem(f"{name}_ext", planes + 2, tall, LANES)
        for part in ("yf", "yl", "yhi", "ylo"):
            vmem(f"{name}_{part}", planes, 1, LANES)
        for part in ("px", "xlo", "xhi", "side"):
            vmem(f"{name}_{part}", tall, LANES)
    vmem("f0", 6, 16, 32, LANES)
    vmem("d0", 16, 32, LANES)
    vmem("t0", 32, LANES)
    vmem("t1w", 64, LANES)
    vmem("k1", 8, 16, LANES)
    for level, (planes, rows, _) in RING.items():
        for kind in "wsvced":
            vmem(f"{kind}{level}", planes, rows, LANES)
        vmem(f"f{level}", 6, planes, rows, LANES)
        vmem(f"t{level}", rows, LANES)
    for name in ("w1", "s1"):
        vmem(f"{name}_px", 16, LANES)
        vmem(f"{name}_pairs", 4, 16, LANES)
        vmem(f"{name}_land", 3, 4, 32, LANES)
        vmem(f"{name}_left", 3, 32, LANES)
        vmem(f"{name}_right", 3, 32, LANES)
    vmem("s4", 1, 4, LANES)
    vmem("source", 16, 32, LANES)
    vmem("weight", 16, 32, LANES)
    vmem("out", 16, 32, LANES)
    vmem("residual", 16, 32, LANES)
    for level, rows in ((2, 8), (3, 4), (4, 2)):
        vmem(f"h{level}", 16 >> level, rows, LANES)
        vmem(f"u{level - 1}", 2 * rows, LANES)
    vmem("own3", 8, LANES)
    vmem("side3", 26, 8, LANES)
    for level, (planes, rows, _) in zip((4, 5, 6), COARSE):
        tall = padded_rows(rows)
        for kind in "wvc":
            vmem(f"{kind}{level}_ext", planes + 2, tall, LANES)
        vmem(f"f{level}", 6, planes, tall, LANES)
        vmem(f"d{level}", planes, tall, LANES)
        vmem(f"q{level}", planes, tall, LANES)
        vmem(f"e{level}", planes, tall, LANES)
        vmem(f"t{level}", tall, LANES)
        if level > 4:
            vmem(f"k{level}", planes, tall, LANES)
    for kind in "ws":
        vmem(f"g0{kind}", 1, LANES)
        vmem(f"g1{kind}", size["gy"], size["gx"], 1, LANES)
        vmem(f"g2{kind}", 8, LANES)
        vmem(f"g5{kind}", size["gz"], 8, LANES)
    vmem("g6", size["gx"] * size["gz"], 2 * LANES)
    shapes["load"] = pltpu.SemaphoreType.DMA((5,))
    shapes["send"] = pltpu.SemaphoreType.DMA((len(SWAP_FIELDS), 6))
    shapes["recv"] = pltpu.SemaphoreType.DMA((len(SWAP_FIELDS), 6))
    shapes["send_side"] = pltpu.SemaphoreType.DMA((2, 26))
    shapes["recv_side"] = pltpu.SemaphoreType.DMA((2, 26))
    counts = [("side3", 26)]
    for kind in "ws":
        counts += [(f"flat_{kind}", size["gx"] * size["gy"]), (f"gz_{kind}", size["gz"])]
    for key, count in counts:
        shapes[f"send_{key}"] = pltpu.SemaphoreType.DMA((count,))
        shapes[f"recv_{key}"] = pltpu.SemaphoreType.DMA((count,))
    return shapes


def solution(mesh):
    size = dict(mesh.shape)
    spec = P("gz", "gx", "gy")

    def body(source, conductivity):
        shapes = buffers(size)
        block = jax.ShapeDtypeStruct(source.shape, F32)

        def run(*refs):
            kernel(size, tuple(shapes), *refs)

        return pl.pallas_call(
            run,
            out_shape=(block, block),
            in_specs=[pl.BlockSpec(memory_space=pltpu.HBM)] * 2,
            out_specs=[pl.BlockSpec(memory_space=pltpu.HBM)] * 2,
            scratch_shapes=list(shapes.values()),
            compiler_params=pltpu.CompilerParams(
                collective_id=0, has_side_effects=True, vmem_limit_bytes=63 * 1024 * 1024
            ),
        )(source, conductivity)

    return jax.shard_map(
        body, mesh=mesh, in_specs=(spec, spec), out_specs=(spec, spec), check_vma=False
    )
```
